32 devices in a mesh: samples: 2 (over x), brick: 16 (over z, y, core).
Axes of the slice: x: 2, y: 2, z: 4, core: 2. Of those that a mesh axis runs over, the one named last changes fastest.
Arguments:
- source: float32 [128, 128, 256], P(('samples', 'brick')), parts along dimension 0, may hold values from -6 to 6
- guess: float32 [128, 128, 256], P(('samples', 'brick')), parts along dimension 0, may hold values from -6 to 6
- log_perm: float32 [128, 128, 256], P(('samples', 'brick')), parts along dimension 0, may hold values from -3 to 3
- owner: int32 [16], replicated, may hold values from 0 to 15, each once
Outputs:
- corrected: float32 [128, 128, 256], P(('samples', 'brick')), parts along dimension 0
- coarse_held: float32 [32, 2048], P(('samples', 'brick')), parts along dimension 0
The draws below stay inside these ranges and needn't reach their ends.
There are 2 independent parts, one for each index of `samples`. The reference program is written for one: setup_inputs(seed, part) draws one part's arguments, and reference() takes and returns one part's arrays. A program takes and returns all parts, laid end to end along the dimension named above; an argument that names none is the same for every part. Nothing has to cross between parts.
Inputs may be any that keep to these rules, and one draw needn't show every extreme that they name: `owner`: each brick index appears exactly once.
All inputs are finite; a program needn't handle non-finite values.
Results may differ from the reference program's by a relative error of at most 0.00005.
Values sent between devices are 32-bit elements; how exact they have to be, the bound alone decides.
A program may use at most 64 MiB of HBM per device.

```python
import jax
import jax.numpy as jnp
from jax import lax

NY = 128
NZ = 256
NU = 2
SWEEPS = 8
NX = 64
CPD = 1
BLOCKS = 16
NXC = 16
CYC = 32
CZC = 64


def channel_columns(key):
    key_mask = jax.random.fold_in(key, 7)
    column_mask = jax.random.uniform(key_mask, (NY // 4, NZ // 4)) < 0.35
    column_mask = jnp.repeat(jnp.repeat(column_mask, 4, axis=0), 4, axis=1)
    return column_mask


def draw_log_perm(key, part):
    column_mask = channel_columns(key)
    key_rough = jax.random.fold_in(key, 12)
    base_level = jnp.where(column_mask, 0.4, -1.6).astype(jnp.float32)
    rough_part = 0.45 * jax.random.normal(key_rough, (NX, NY, NZ), jnp.float32)
    return jnp.clip(base_level[None, :, :] + rough_part, -3.0, 3.0).astype(jnp.float32)


def draw_source(key, part):
    column_mask = channel_columns(key)
    key_signs = jax.random.fold_in(key, 21)
    key_size = jax.random.fold_in(key, 22)
    key_rough = jax.random.fold_in(key, 23)
    sign_draw = jnp.where(jax.random.uniform(key_signs, (NX // 4,)) < 0.5, -1.0, 1.0).astype(jnp.float32)
    magnitude = jax.random.uniform(key_size, (NX // 4,), jnp.float32, 1.0, 2.5)
    plane_level = sign_draw * magnitude
    rough_part = 0.4 * jax.random.normal(key_rough, (NX, NY, NZ), jnp.float32)
    plane_level = jnp.repeat(plane_level, 4)
    column_weight = jnp.where(column_mask, 1.0, 0.05).astype(jnp.float32)
    smooth_part = plane_level[:, None, None] * column_weight[None, :, :]
    return jnp.clip(smooth_part + rough_part, -6.0, 6.0).astype(jnp.float32)


def block_scale(stream_key, extent, shards, low, largest):
    factor_of, own = 1.0, jax.random.fold_in(stream_key, 6)
    for axis_at, parts in shards:
        heights = jnp.exp(jax.random.uniform(jax.random.fold_in(own, axis_at), (parts,), jnp.float32, low / len(shards), largest / len(shards)))
        factor_of = factor_of * jnp.repeat(heights, extent[axis_at] // parts).reshape([-1 if axis == axis_at else 1 for axis in range(len(extent))])
    return factor_of


def noise(key, dims, deviation, most, shards=(), kind=jnp.bfloat16):
    gain = block_scale(key, dims, shards, -0.22, 0.18) if shards else 1.0
    entries = jax.random.normal(key, dims, jnp.float32) * deviation * gain
    return jnp.minimum(jnp.maximum(entries, -most), most).astype(kind)


def setup_inputs(seed: int = 0, part: int = 0) -> dict:
    keys = jax.random.split(jax.random.key(seed), 5)
    part_keys = jax.random.split(jax.random.fold_in(keys[4], part), 5)
    source = draw_source(jax.random.fold_in(jax.random.fold_in(keys[4], part), 71), part)
    guess = noise(part_keys[1], (NX, NY, NZ), 1.0, 6.0, ((0, 16),), jnp.float32)
    log_perm = draw_log_perm(jax.random.fold_in(jax.random.fold_in(keys[4], part), 71), part)
    owner = jax.random.permutation(keys[3], BLOCKS).astype(jnp.int32)
    return dict(source=source, guess=guess, log_perm=log_perm, owner=owner)


relax_weight = 0.8


def prolong_matrix(n_fine):
    fine_idx = jnp.arange(n_fine)[:, None]
    coarse_idx = jnp.arange(n_fine // 4)[None, :]
    base = fine_idx // 4
    offset = fine_idx % 4
    weight_own = jnp.where((offset == 0) | (offset == 3), 0.625, 0.875).astype(jnp.float32)
    side = jnp.where(offset < 2, -1, 1)
    own = jnp.where(coarse_idx == base, weight_own, 0.0)
    other = jnp.where(coarse_idx == base + side, 1.0 - weight_own, 0.0)
    return (own + other).astype(jnp.float32)


def apply_op(field, coeff):
    padded = jnp.pad(field, 1)
    kpad = jnp.pad(coeff, 1)
    center = padded[1:-1, 1:-1, 1:-1]
    kcen = kpad[1:-1, 1:-1, 1:-1]
    pairs = [
        (padded[:-2, 1:-1, 1:-1], kpad[:-2, 1:-1, 1:-1]),
        (padded[2:, 1:-1, 1:-1], kpad[2:, 1:-1, 1:-1]),
        (padded[1:-1, :-2, 1:-1], kpad[1:-1, :-2, 1:-1]),
        (padded[1:-1, 2:, 1:-1], kpad[1:-1, 2:, 1:-1]),
        (padded[1:-1, 1:-1, :-2], kpad[1:-1, 1:-1, :-2]),
        (padded[1:-1, 1:-1, 2:], kpad[1:-1, 1:-1, 2:]),
    ]
    diagonal = jnp.zeros_like(field)
    nearby = jnp.zeros_like(field)
    for value, kval in pairs:
        face = 0.5 * (kcen + kval)
        diagonal = diagonal + face
        nearby = nearby + face * value
    return diagonal * center - nearby, diagonal


def reference(source, guess, log_perm, owner):
    hp = lax.Precision.HIGHEST
    perm = jnp.exp(log_perm)
    smooth = guess
    for sweep in range(NU):
        image, diagonal = apply_op(smooth, perm)
        smooth = smooth + relax_weight * (source - image) / diagonal
    image, diagonal = apply_op(smooth, perm)
    resid = source - image
    px = prolong_matrix(NX)
    py = prolong_matrix(NY)
    pz = prolong_matrix(NZ)
    step_one = jnp.einsum('xyz,xX->Xyz', resid, px, precision=hp)
    step_two = jnp.einsum('Xyz,yY->XYz', step_one, py, precision=hp)
    coarse_rhs = jnp.einsum('XYz,zZ->XYZ', step_two, pz, precision=hp) * (1.0 / 64.0)
    coarse_perm = perm.reshape(NXC, 4, CYC, 4, CZC, 4).sum(axis=(1, 3, 5)) * (1.0 / 64.0)
    coarse = jnp.zeros((NXC, CYC, CZC), jnp.float32)
    for sweep in range(SWEEPS):
        image, diagonal = apply_op(coarse, coarse_perm)
        coarse = coarse + relax_weight * (coarse_rhs - image * (1.0 / 16.0)) / (diagonal * (1.0 / 16.0))
    back_one = jnp.einsum('XYZ,xX->xYZ', coarse, px, precision=hp)
    back_two = jnp.einsum('xYZ,yY->xyZ', back_one, py, precision=hp)
    correction = jnp.einsum('xyZ,zZ->xyz', back_two, pz, precision=hp)
    corrected = smooth + correction
    blocks = coarse.reshape(BLOCKS, CPD, CYC * CZC)
    held = jnp.zeros_like(blocks).at[owner].set(blocks)
    return corrected, held.reshape(NXC, CYC * CZC)
```

```python
import functools

import jax
import jax.numpy as jnp
import ml_dtypes
import numpy as np
from jax import lax
from jax.experimental import pallas as pl
from jax.experimental.pallas import tpu as pltpu
from jax.sharding import PartitionSpec as P

SWEEPS = 8
CHUNKS = 4
MESH = pl.DeviceIdType.MESH
F32 = jnp.float32
BF16 = jnp.bfloat16


def prolong_matrix(n_fine):
    i = np.arange(n_fine)[:, None]
    j = np.arange(n_fine // 4)[None, :]
    base, offset = i // 4, i % 4
    own = np.where((offset == 0) | (offset == 3), 0.625, 0.875)
    side = np.where(offset < 2, -1, 1)
    return np.where(j == base, own, 0.0) + np.where(j == base + side, 1.0 - own, 0.0)


def mean_matrix(n_fine):
    i = np.arange(n_fine)[:, None]
    j = np.arange(n_fine // 4)[None, :]
    return np.where(j == i // 4, 1.0, 0.0)


def even_odd(m):
    return np.concatenate([m[:, 0::2], m[:, 1::2]], axis=1)


def halves(m):
    zero = np.zeros_like(m)
    return np.stack([np.concatenate([m, zero], 1), np.concatenate([zero, m], 1)])


def split(x):
    hi = x.astype(BF16)
    return hi, (x - hi.astype(F32)).astype(BF16)


def dot(a, b):
    return jnp.dot(a, b, preferred_element_type=F32)


def to_coarse(y_mat, z_mat, x):
    hi, lo = split(x)
    a = dot(y_mat, hi) + dot(y_mat, lo)
    hi, lo = split(a)
    h = a.shape[0] // 2
    return (
        dot(hi[:h], z_mat[0]) + dot(lo[:h], z_mat[0]) + dot(hi[h:], z_mat[1]) + dot(lo[h:], z_mat[1])
    )


def smooth_kernel(
    n, ny, nz,
    source_hbm, guess_hbm, logq_hbm, ry, rz, my, mz,
    smooth, all_rhs, all_q,
    src, logq, K, U0, U1, U2, D, N, EK, X, H, own, part,
    local_sem, halo_send, halo_recv, part_send, part_recv, q_send, q_recv, r_send, r_recv,
):
    me = lax.axis_index("brick")
    R = ny // CHUNKS
    has = (me > 0, me < n - 1)
    peer_of = (me - 1, me + 1)

    loads = [
        pltpu.make_async_copy(logq_hbm, logq, local_sem.at[0]),
        pltpu.make_async_copy(guess_hbm, U0.at[pl.ds(1, 4), pl.ds(8, ny)], local_sem.at[1]),
        pltpu.make_async_copy(source_hbm, src, local_sem.at[2]),
    ]
    for copy in loads:
        copy.start()

    barrier = pltpu.get_barrier_semaphore()

    def greet(k, _):
        pl.semaphore_signal(
            barrier, inc=1, device_id={"brick": lax.rem(me + k, n)}, device_id_type=MESH
        )
        return 0

    lax.fori_loop(1, n, greet, 0)
    pl.semaphore_wait(barrier, n - 1)

    def halo(which, side, c):
        plane = 3 * side
        start = c * R if isinstance(c, int) else pl.multiple_of(c * R, R)
        rows = pl.ds(start, R)
        if which == 2:
            ref = U1.at[plane + 1, pl.ds(start + 8, R)]
        else:
            ref = (logq_hbm, guess_hbm)[which].at[plane, rows]
        return pltpu.make_async_remote_copy(
            src_ref=ref,
            dst_ref=H.at[which, 1 - side, rows],
            send_sem=halo_send.at[which, side, c],
            recv_sem=halo_recv.at[which, 1 - side, c],
            device_id={"brick": peer_of[side]},
            device_id_type=MESH,
        )

    def arrival(which, side, c):
        start = c * R if isinstance(c, int) else pl.multiple_of(c * R, R)
        ref = H.at[which, side, pl.ds(start, R)]
        return pltpu.make_async_remote_copy(
            src_ref=ref,
            dst_ref=ref,
            send_sem=halo_send.at[which, side, c],
            recv_sem=halo_recv.at[which, side, c],
            device_id={"brick": peer_of[side]},
            device_id_type=MESH,
        )

    for c in range(CHUNKS):
        for side in range(2):

            @pl.when(has[side])
            def _():
                halo(0, side, c).start()
                halo(1, side, c).start()

    zero_plane = jnp.zeros((ny + 16, nz), F32)
    zero_rows = jnp.zeros((8, nz), F32)
    for ref in (K, U0, U1, U2):
        ref[0] = zero_plane
        ref[5] = zero_plane
        for p in range(1, 5):
            ref[p, 0:8] = zero_rows
            ref[p, ny + 8 : ny + 16] = zero_rows

    lane = lax.broadcasted_iota(jnp.int32, (R, nz), 1)
    first, last = lane == 0, lane == nz - 1

    def yz(window):
        center = window[8 : R + 8]
        low = jnp.where(first, 0.0, pltpu.roll(center, 1, 1))
        high = jnp.where(last, 0.0, pltpu.roll(center, nz - 1, 1))
        return (window[7 : R + 7] + window[9 : R + 9]) + (low + high)

    loads[0].wait()

    def exps(i, _):
        p, start = i // CHUNKS, pl.multiple_of((i % CHUNKS) * R, R)
        K[p + 1, pl.ds(start + 8, R)] = jnp.exp(logq[p, pl.ds(start, R)])
        return 0

    lax.fori_loop(0, 4 * CHUNKS, exps, 0)
    loads[1].wait()
    loads[2].wait()

    def nearby(U, p, start):
        at = pl.ds(start + 8, R)
        window = pl.ds(start, R + 16)
        u, k = U[p + 1, window], K[p + 1, window]
        um, up, km, kp = U[p, at], U[p + 2, at], K[p, at], K[p + 2, at]
        su = yz(u) + (um + up)
        sku = yz(u * k) + (km * um + kp * up)
        q = k[8 : R + 8]
        return u[8 : R + 8], q, k, km + kp, 0.5 * (q * su + sku)

    def sweep_one(i, _):
        p, start = i // CHUNKS, pl.multiple_of((i % CHUNKS) * R, R)
        rows = pl.ds(start, R)
        u, q, k, kx, near = nearby(U0, p, start)
        d = 3.0 * q + 0.5 * (yz(k) + kx)
        total = src[p, rows] + near
        D[p, rows] = d
        N[p, rows] = total
        U1[p + 1, pl.ds(start + 8, R)] = 0.2 * u + 0.8 * total / d
        return 0

    lax.fori_loop(0, 4 * CHUNKS, sweep_one, 0)

    own[...] = to_coarse(
        my[...], mz, (K[1, 8 : ny + 8] + K[2, 8 : ny + 8]) + (K[3, 8 : ny + 8] + K[4, 8 : ny + 8])
    ) * (1.0 / 64.0)
    all_q[me] = own[...]

    def finish_one(c, _):
        start = pl.multiple_of(c * R, R)
        rows, at = pl.ds(start, R), pl.ds(start + 8, R)
        for side in range(2):
            p = 3 * side

            @pl.when(has[side])
            def _():
                arrival(0, side, c).wait_recv()
                arrival(1, side, c).wait_recv()
                q = K[p + 1, at]
                kh = jnp.exp(H[0, side, rows])
                EK[side, rows] = kh
                D[p, rows] = D[p, rows] + 0.5 * kh
                N[p, rows] = N[p, rows] + 0.5 * (q + kh) * H[1, side, rows]

            @pl.when(jnp.logical_not(has[side]))
            def _():
                EK[side, rows] = jnp.zeros((R, nz), F32)

            U1[p + 1, at] = 0.2 * U0[p + 1, at] + 0.8 * N[p, rows] / D[p, rows]

            @pl.when(has[side])
            def _():
                halo(2, side, c).start()

        return 0

    lax.fori_loop(0, CHUNKS, finish_one, 0)

    def spread(ref, k, send, recv):
        return pltpu.make_async_remote_copy(
            src_ref=ref.at[me],
            dst_ref=ref.at[me],
            send_sem=send.at[k],
            recv_sem=recv.at[me],
            device_id={"brick": lax.rem(me + k, n)},
            device_id_type=MESH,
        )

    def landed(ref, k, send, recv):
        who = lax.rem(me + k, n)
        return pltpu.make_async_remote_copy(
            src_ref=ref.at[who],
            dst_ref=ref.at[who],
            send_sem=send.at[k],
            recv_sem=recv.at[who],
            device_id={"brick": who},
            device_id_type=MESH,
        )

    def send_q(k, _):
        spread(all_q, k, q_send, q_recv).start()
        return 0

    lax.fori_loop(1, n, send_q, 0)

    def sweep_two(i, _):
        p, start = i // CHUNKS, pl.multiple_of((i % CHUNKS) * R, R)
        rows = pl.ds(start, R)
        u, q, k, kx, near = nearby(U1, p, start)
        total = src[p, rows] + near
        N[p, rows] = total
        U2[p + 1, pl.ds(start + 8, R)] = 0.2 * u + 0.8 * total / D[p, rows]
        return 0

    lax.fori_loop(0, 4 * CHUNKS, sweep_two, 0)

    def finish_two(c, _):
        start = pl.multiple_of(c * R, R)
        rows, at = pl.ds(start, R), pl.ds(start + 8, R)
        for side in range(2):
            p = 3 * side

            @pl.when(has[side])
            def _():
                arrival(2, side, c).wait_recv()
                total = N[p, rows] + 0.5 * (K[p + 1, at] + EK[side, rows]) * H[2, side, rows]
                U2[p + 1, at] = 0.2 * U1[p + 1, at] + 0.8 * total / D[p, rows]

        return 0

    lax.fori_loop(0, CHUNKS, finish_two, 0)

    present = [jnp.where(flag, 0.5, 0.0).astype(F32) for flag in has]

    def residual(c, _):
        start = pl.multiple_of(c * R, R)
        rows, at = pl.ds(start, R), pl.ds(start + 8, R)

        def row(p):
            u, q, k, kx, near = nearby(U2, p, start)
            smooth[p, rows] = u
            return src[p, rows] - D[p, rows] * u + near

        r0, r1 = row(0), row(1)
        flo = present[0] * (K[1, at] + EK[0, rows]) * U2[1, at]
        X[0, rows] = 0.625 * flo + 0.375 * r0 + 0.125 * r1
        X[1, rows] = 0.375 * flo + 0.625 * r0 + 0.875 * r1
        r2, r3 = row(2), row(3)
        fhi = present[1] * (K[4, at] + EK[1, rows]) * U2[4, at]
        X[2, rows] = 0.625 * fhi + 0.375 * r3 + 0.125 * r2
        X[1, rows] = X[1, rows] + (0.375 * fhi + 0.625 * r3 + 0.875 * r2)
        return 0

    lax.fori_loop(0, CHUNKS, residual, 0)

    def partial(side):
        return pltpu.make_async_remote_copy(
            src_ref=part.at[side],
            dst_ref=part.at[3 - side],
            send_sem=part_send.at[side],
            recv_sem=part_recv.at[1 - side],
            device_id={"brick": peer_of[side]},
            device_id_type=MESH,
        )

    def partial_in(side):
        return pltpu.make_async_remote_copy(
            src_ref=part.at[2 + side],
            dst_ref=part.at[2 + side],
            send_sem=part_send.at[side],
            recv_sem=part_recv.at[side],
            device_id={"brick": peer_of[side]},
            device_id_type=MESH,
        )

    for side in range(2):
        part[side] = to_coarse(ry[...], rz, X[2 * side])

    for side in range(2):

        @pl.when(has[side])
        def _():
            partial(side).start()

    own[...] = to_coarse(ry[...], rz, X[1])
    for side in range(2):

        @pl.when(has[side])
        def _():
            partial_in(side).wait_recv()
            own[...] = own[...] + part[2 + side]

    all_rhs[me] = own[...] * (1.0 / 64.0)

    def send_r(k, _):
        spread(all_rhs, k, r_send, r_recv).start()
        return 0

    lax.fori_loop(1, n, send_r, 0)

    def settle(k, _):
        landed(all_q, k, q_send, q_recv).wait_recv()
        landed(all_rhs, k, r_send, r_recv).wait_recv()
        spread(all_q, k, q_send, q_recv).wait_send()
        spread(all_rhs, k, r_send, r_recv).wait_send()
        return 0

    for side in range(2):

        @pl.when(has[side])
        def _():
            for c in range(CHUNKS):
                for which in range(3):
                    halo(which, side, c).wait_send()
            partial(side).wait_send()

    lax.fori_loop(1, n, settle, 0)


def coarse_kernel(
    n, group,
    owner, rhs, perm, smooth, ez, ey,
    corrected, held,
    q_pad, C, coef, B,
):
    me = lax.axis_index("brick")
    rows, lanes = rhs.shape[1:]
    cz = lanes // 2
    shape = (group, rows, lanes)
    row = lax.broadcasted_iota(jnp.int32, shape, 1)
    lane = lax.broadcasted_iota(jnp.int32, shape, 2)
    low_half = lane < cz
    z = jnp.where(low_half, lane, lane - cz)
    y_first = (row == 0) & low_half
    y_last = (row == rows - 1) & jnp.logical_not(low_half)
    z_first, z_last = z == 0, z == cz - 1

    def shifts(c):
        swapped = pltpu.roll(c, cz, 2)
        y_low = jnp.where(low_half, pltpu.roll(swapped, 1, 1), swapped)
        y_high = jnp.where(low_half, swapped, pltpu.roll(swapped, rows - 1, 1))
        return y_low, y_high, pltpu.roll(c, 1, 2), pltpu.roll(c, lanes - 1, 2)

    edge = jnp.zeros((rows, lanes), F32)
    q_pad[0] = edge
    q_pad[n + 1] = edge
    for slot in range(2):
        C[slot, 0] = edge
        C[slot, n + 1] = edge
    q_pad[1 : n + 1] = perm[...]

    def prepare(g, _):
        at = pl.multiple_of(g * group, group)
        q = q_pad[pl.ds(at + 1, group)]
        near = [q_pad[pl.ds(at, group)], q_pad[pl.ds(at + 2, group)]]
        near += [
            jnp.where(out, 0.0, v)
            for out, v in zip((y_first, y_last, z_first, z_last), shifts(q))
        ]
        faces = [0.5 * (q + v) for v in near]
        diagonal = ((faces[0] + faces[1]) + (faces[2] + faces[3])) + (faces[4] + faces[5])
        scale = 0.8 / diagonal
        for k, out in enumerate((None, None, y_first, y_last, z_first, z_last)):
            f = faces[k] * scale
            coef[k, pl.ds(at, group)] = f if out is None else jnp.where(out, 0.0, f)
        b = 16.0 * rhs[pl.ds(at, group)] * scale
        B[pl.ds(at, group)] = b
        C[0, pl.ds(at + 1, group)] = b
        return 0

    lax.fori_loop(0, n // group, prepare, 0)

    for sweep in range(SWEEPS - 1):
        now, later = sweep % 2, 1 - sweep % 2

        def step(g, _):
            at = pl.multiple_of(g * group, group)
            c = C[now, pl.ds(at + 1, group)]
            near = (C[now, pl.ds(at, group)], C[now, pl.ds(at + 2, group)]) + shifts(c)
            terms = [coef[k, pl.ds(at, group)] * v for k, v in enumerate(near)]
            total = B[pl.ds(at, group)] + 0.2 * c
            total = (total + (terms[0] + terms[1])) + ((terms[2] + terms[3]) + (terms[4] + terms[5]))
            C[later, pl.ds(at + 1, group)] = total
            return 0

        lax.fori_loop(0, n // group, step, 0)

    final = (SWEEPS - 1) % 2

    mine = jnp.zeros((rows, lanes), F32)
    for b in range(n):
        mine = jnp.where(owner[b] == me, C[final, b + 1], mine)
    for r in range(rows):
        held[0:1, r * lanes : (r + 1) * lanes] = mine[r : r + 1]

    below, mid, above = C[final, me], C[final, me + 1], C[final, me + 2]
    planes = jnp.concatenate(
        [
            0.625 * mid + 0.375 * below,
            0.875 * mid + 0.125 * below,
            0.875 * mid + 0.125 * above,
            0.625 * mid + 0.375 * above,
        ],
        axis=0,
    )
    hi, lo = split(planes)
    even = dot(hi, ez[0]) + dot(lo, ez[0])
    odd = dot(hi, ez[1]) + dot(lo, ez[1])
    for p in range(4):
        both = jnp.concatenate(
            [even[p * rows : (p + 1) * rows], odd[p * rows : (p + 1) * rows]], axis=0
        )
        hi, lo = split(both)
        corrected[p] = smooth[p] + (dot(ey[...], hi) + dot(ey[...], lo))


def local(n, source, guess, log_perm, owner):
    planes, ny, nz = source.shape
    assert planes == 4
    cells = (ny // 4) * (nz // 4)
    rows, lanes = ny // 8, nz // 2
    dense = (rows, lanes)
    as_bf16 = lambda m: jnp.asarray(m.astype(ml_dtypes.bfloat16))
    py, pz = even_odd(prolong_matrix(ny)), prolong_matrix(nz)
    ry, rz = as_bf16(py.T), as_bf16(halves(pz))
    my, mz = as_bf16(even_odd(mean_matrix(ny)).T), as_bf16(halves(mean_matrix(nz)))
    ey, ez = as_bf16(py), as_bf16(halves(pz).transpose(0, 2, 1))
    vmem = pl.BlockSpec(memory_space=pltpu.VMEM)
    anywhere = pl.BlockSpec(memory_space=pl.ANY)
    whole = lambda *s: pltpu.VMEM(s, F32)
    dma = lambda *s: pltpu.SemaphoreType.DMA(s)
    padded = (6, ny + 16, nz)
    smooth, all_rhs, all_q = pl.pallas_call(
        functools.partial(smooth_kernel, n, ny, nz),
        out_shape=(
            jax.ShapeDtypeStruct((4, ny, nz), F32),
            jax.ShapeDtypeStruct((n,) + dense, F32),
            jax.ShapeDtypeStruct((n,) + dense, F32),
        ),
        in_specs=[anywhere] * 3 + [vmem] * 4,
        out_specs=(vmem,) * 3,
        scratch_shapes=[
            whole(4, ny, nz), whole(4, ny, nz),
            whole(*padded), whole(*padded), whole(*padded), whole(*padded),
            whole(4, ny, nz), whole(4, ny, nz),
            whole(2, ny, nz), whole(3, ny, nz), whole(3, 2, ny, nz),
            whole(*dense), whole(4, *dense),
            dma(3), dma(3, 2, CHUNKS), dma(3, 2, CHUNKS), dma(2), dma(2),
            dma(n), dma(n), dma(n), dma(n),
        ],
        compiler_params=pltpu.CompilerParams(
            collective_id=0, has_side_effects=True, vmem_limit_bytes=24 * 2**20
        ),
        name="smooth",
    )(source, guess, log_perm, ry, rz, my, mz)
    return pl.pallas_call(
        functools.partial(coarse_kernel, n, min(8, n)),
        out_shape=(
            jax.ShapeDtypeStruct((4, ny, nz), F32),
            jax.ShapeDtypeStruct((1, cells), F32),
        ),
        in_specs=[pl.BlockSpec(memory_space=pltpu.SMEM)] + [vmem] * 5,
        out_specs=(vmem, vmem),
        scratch_shapes=[
            whole(n + 2, *dense), whole(2, n + 2, *dense), whole(6, n, *dense), whole(n, *dense),
        ],
        compiler_params=pltpu.CompilerParams(vmem_limit_bytes=24 * 2**20),
        name="coarse",
    )(owner, all_rhs, all_q, smooth, ez, ey)


def solution(mesh):
    spec = P(("samples", "brick"), None, None)
    return jax.shard_map(
        functools.partial(local, mesh.shape["brick"]),
        mesh=mesh,
        in_specs=(spec, spec, spec, P()),
        out_specs=(spec, P(("samples", "brick"), None)),
        check_vma=False,
    )
```

```python
import functools

import jax
import jax.numpy as jnp
import ml_dtypes
import numpy as np
from jax import lax
from jax.experimental import pallas as pl
from jax.experimental.pallas import tpu as pltpu
from jax.sharding import PartitionSpec as P

SWEEPS = 8
CHUNKS = 4
MESH = pl.DeviceIdType.MESH
F32 = jnp.float32
BF16 = jnp.bfloat16


def prolong_matrix(n_fine):
    i = np.arange(n_fine)[:, None]
    j = np.arange(n_fine // 4)[None, :]
    base, offset = i // 4, i % 4
    own = np.where((offset == 0) | (offset == 3), 0.625, 0.875)
    side = np.where(offset < 2, -1, 1)
    return np.where(j == base, own, 0.0) + np.where(j == base + side, 1.0 - own, 0.0)


def mean_matrix(n_fine):
    i = np.arange(n_fine)[:, None]
    j = np.arange(n_fine // 4)[None, :]
    return np.where(j == i // 4, 1.0, 0.0)


def even_odd(m):
    return np.concatenate([m[:, 0::2], m[:, 1::2]], axis=1)


def halves(m):
    zero = np.zeros_like(m)
    return np.stack([np.concatenate([m, zero], 1), np.concatenate([zero, m], 1)])


def split(x):
    hi = x.astype(BF16)
    return hi, (x - hi.astype(F32)).astype(BF16)


def dot(a, b):
    return jnp.dot(a, b, preferred_element_type=F32)


def to_coarse(y_mat, z_mat, x):
    hi, lo = split(x)
    a = dot(y_mat, hi) + dot(y_mat, lo)
    hi, lo = split(a)
    h = a.shape[0] // 2
    return (
        dot(hi[:h], z_mat[0]) + dot(lo[:h], z_mat[0]) + dot(hi[h:], z_mat[1]) + dot(lo[h:], z_mat[1])
    )


def smooth_kernel(
    n, ny, nz,
    source_hbm, guess_hbm, logq_hbm, ry_hbm, rz_hbm, my_hbm, mz_hbm,
    smooth_hbm, all_rhs, coef_hbm, scaled_hbm,
    coef, scaled, ry, rz, my, mz, all_q, q_pad, src, logq, K, U0, U1, U2, D, N, EK, X, H, own, part,
    local_sem, halo_send, halo_recv, part_send, part_recv, q_send, q_recv, r_send, r_recv,
):
    me = lax.axis_index("brick")
    R = ny // CHUNKS
    has = (me > 0, me < n - 1)
    peer_of = (me - 1, me + 1)

    loads = [
        pltpu.make_async_copy(logq_hbm, logq, local_sem.at[0]),
        pltpu.make_async_copy(guess_hbm, U0.at[pl.ds(1, 4), pl.ds(8, ny)], local_sem.at[1]),
        pltpu.make_async_copy(source_hbm, src, local_sem.at[2]),
        pltpu.make_async_copy(my_hbm, my, local_sem.at[3]),
        pltpu.make_async_copy(mz_hbm, mz, local_sem.at[4]),
        pltpu.make_async_copy(ry_hbm, ry, local_sem.at[5]),
        pltpu.make_async_copy(rz_hbm, rz, local_sem.at[6]),
    ]
    for copy in loads:
        copy.start()

    barrier = pltpu.get_barrier_semaphore()

    def greet(k, _):
        pl.semaphore_signal(
            barrier, inc=1, device_id={"brick": lax.rem(me + k, n)}, device_id_type=MESH
        )
        return 0

    lax.fori_loop(1, n, greet, 0)
    pl.semaphore_wait(barrier, n - 1)

    def halo(which, side, c):
        plane = 3 * side
        start = c * R if isinstance(c, int) else pl.multiple_of(c * R, R)
        rows = pl.ds(start, R)
        if which == 2:
            ref = U1.at[plane + 1, pl.ds(start + 8, R)]
        else:
            ref = (logq_hbm, guess_hbm)[which].at[plane, rows]
        return pltpu.make_async_remote_copy(
            src_ref=ref,
            dst_ref=H.at[which, 1 - side, rows],
            send_sem=halo_send.at[which, side, c],
            recv_sem=halo_recv.at[which, 1 - side, c],
            device_id={"brick": peer_of[side]},
            device_id_type=MESH,
        )

    def arrival(which, side, c):
        start = c * R if isinstance(c, int) else pl.multiple_of(c * R, R)
        ref = H.at[which, side, pl.ds(start, R)]
        return pltpu.make_async_remote_copy(
            src_ref=ref,
            dst_ref=ref,
            send_sem=halo_send.at[which, side, c],
            recv_sem=halo_recv.at[which, side, c],
            device_id={"brick": peer_of[side]},
            device_id_type=MESH,
        )

    for c in range(CHUNKS):
        for side in range(2):

            @pl.when(has[side])
            def _():
                halo(0, side, c).start()
                halo(1, side, c).start()

    zero_plane = jnp.zeros((ny + 16, nz), F32)
    zero_rows = jnp.zeros((8, nz), F32)
    for ref in (K, U0, U1, U2):
        ref[0] = zero_plane
        ref[5] = zero_plane
        for p in range(1, 5):
            ref[p, 0:8] = zero_rows
            ref[p, ny + 8 : ny + 16] = zero_rows

    lane = lax.broadcasted_iota(jnp.int32, (R, nz), 1)
    first, last = lane == 0, lane == nz - 1

    def yz(window):
        center = window[8 : R + 8]
        low = jnp.where(first, 0.0, pltpu.roll(center, 1, 1))
        high = jnp.where(last, 0.0, pltpu.roll(center, nz - 1, 1))
        return (window[7 : R + 7] + window[9 : R + 9]) + (low + high)

    loads[0].wait()

    def exps(i, _):
        p, start = i // CHUNKS, pl.multiple_of((i % CHUNKS) * R, R)
        K[p + 1, pl.ds(start + 8, R)] = jnp.exp(logq[p, pl.ds(start, R)])
        return 0

    lax.fori_loop(0, 4 * CHUNKS, exps, 0)
    for copy in loads[1:]:
        copy.wait()

    def nearby(U, p, start):
        at = pl.ds(start + 8, R)
        window = pl.ds(start, R + 16)
        u, k = U[p + 1, window], K[p + 1, window]
        um, up, km, kp = U[p, at], U[p + 2, at], K[p, at], K[p + 2, at]
        su = yz(u) + (um + up)
        sku = yz(u * k) + (km * um + kp * up)
        q = k[8 : R + 8]
        return u[8 : R + 8], q, k, km + kp, 0.5 * (q * su + sku)

    def sweep_one(i, _):
        p, start = i // CHUNKS, pl.multiple_of((i % CHUNKS) * R, R)
        rows = pl.ds(start, R)
        u, q, k, kx, near = nearby(U0, p, start)
        d = 3.0 * q + 0.5 * (yz(k) + kx)
        total = src[p, rows] + near
        D[p, rows] = d
        N[p, rows] = total
        U1[p + 1, pl.ds(start + 8, R)] = 0.2 * u + 0.8 * total / d
        return 0

    lax.fori_loop(0, 4 * CHUNKS, sweep_one, 0)

    own[...] = to_coarse(
        my[...], mz, (K[1, 8 : ny + 8] + K[2, 8 : ny + 8]) + (K[3, 8 : ny + 8] + K[4, 8 : ny + 8])
    ) * (1.0 / 64.0)
    all_q[me] = own[...]

    def finish_one(c, _):
        start = pl.multiple_of(c * R, R)
        rows, at = pl.ds(start, R), pl.ds(start + 8, R)
        for side in range(2):
            p = 3 * side

            @pl.when(has[side])
            def _():
                arrival(0, side, c).wait_recv()
                arrival(1, side, c).wait_recv()
                q = K[p + 1, at]
                kh = jnp.exp(H[0, side, rows])
                EK[side, rows] = kh
                D[p, rows] = D[p, rows] + 0.5 * kh
                N[p, rows] = N[p, rows] + 0.5 * (q + kh) * H[1, side, rows]

            @pl.when(jnp.logical_not(has[side]))
            def _():
                EK[side, rows] = jnp.zeros((R, nz), F32)

            U1[p + 1, at] = 0.2 * U0[p + 1, at] + 0.8 * N[p, rows] / D[p, rows]

            @pl.when(has[side])
            def _():
                halo(2, side, c).start()

        return 0

    def spread(block, ref, k, send, recv):
        return pltpu.make_async_remote_copy(
            src_ref=block,
            dst_ref=ref.at[me],
            send_sem=send.at[k],
            recv_sem=recv.at[me],
            device_id={"brick": lax.rem(me + k, n)},
            device_id_type=MESH,
        )

    def landed(ref, k, send, recv):
        who = lax.rem(me + k, n)
        return pltpu.make_async_remote_copy(
            src_ref=ref.at[who],
            dst_ref=ref.at[who],
            send_sem=send.at[k],
            recv_sem=recv.at[who],
            device_id={"brick": who},
            device_id_type=MESH,
        )

    def send_q(k, _):
        spread(all_q.at[me], all_q, k, q_send, q_recv).start()
        return 0

    def sweep_two(p, start):
        rows = pl.ds(start, R)
        u, q, k, kx, near = nearby(U1, p, start)
        total = src[p, rows] + near
        N[p, rows] = total
        U2[p + 1, pl.ds(start + 8, R)] = 0.2 * u + 0.8 * total / D[p, rows]
        return 0

    def first_stage(c, _):
        @pl.when(c < CHUNKS)
        def _():
            finish_one(c, 0)

        @pl.when(c == CHUNKS - 1)
        def _():
            lax.fori_loop(1, n, send_q, 0)

        @pl.when(c > 0)
        def _():
            start = pl.multiple_of((c - 1) * R, R)
            lax.fori_loop(0, 4, lambda p, _: sweep_two(p, start), 0)

        return 0

    lax.fori_loop(0, CHUNKS + 1, first_stage, 0)

    def finish_two(c, _):
        start = pl.multiple_of(c * R, R)
        rows, at = pl.ds(start, R), pl.ds(start + 8, R)
        for side in range(2):
            p = 3 * side

            @pl.when(has[side])
            def _():
                arrival(2, side, c).wait_recv()
                total = N[p, rows] + 0.5 * (K[p + 1, at] + EK[side, rows]) * H[2, side, rows]
                U2[p + 1, at] = 0.2 * U1[p + 1, at] + 0.8 * total / D[p, rows]

        return 0

    present = [jnp.where(flag, 0.5, 0.0).astype(F32) for flag in has]

    def residual(c, _):
        start = pl.multiple_of(c * R, R)
        rows, at = pl.ds(start, R), pl.ds(start + 8, R)

        def row(p):
            u, q, k, kx, near = nearby(U2, p, start)
            return src[p, rows] - D[p, rows] * u + near

        r0, r1 = row(0), row(1)
        flo = present[0] * (K[1, at] + EK[0, rows]) * U2[1, at]
        X[0, rows] = 0.625 * flo + 0.375 * r0 + 0.125 * r1
        X[1, rows] = 0.375 * flo + 0.625 * r0 + 0.875 * r1
        r2, r3 = row(2), row(3)
        fhi = present[1] * (K[4, at] + EK[1, rows]) * U2[4, at]
        X[2, rows] = 0.625 * fhi + 0.375 * r3 + 0.125 * r2
        X[1, rows] = X[1, rows] + (0.375 * fhi + 0.625 * r3 + 0.875 * r2)
        return 0

    def second_stage(c, _):
        @pl.when(c < CHUNKS)
        def _():
            finish_two(c, 0)

        @pl.when(c > 0)
        def _():
            residual(c - 1, 0)

        return 0

    lax.fori_loop(0, CHUNKS + 1, second_stage, 0)

    stores = [
        pltpu.make_async_copy(U2.at[pl.ds(1, 4), pl.ds(8, ny)], smooth_hbm, local_sem.at[0]),
        pltpu.make_async_copy(own, all_rhs.at[me], local_sem.at[1]),
        pltpu.make_async_copy(coef, coef_hbm, local_sem.at[2]),
        pltpu.make_async_copy(scaled, scaled_hbm, local_sem.at[3]),
    ]
    stores[0].start()

    def partial(side):
        return pltpu.make_async_remote_copy(
            src_ref=part.at[side],
            dst_ref=part.at[3 - side],
            send_sem=part_send.at[side],
            recv_sem=part_recv.at[1 - side],
            device_id={"brick": peer_of[side]},
            device_id_type=MESH,
        )

    def partial_in(side):
        return pltpu.make_async_remote_copy(
            src_ref=part.at[2 + side],
            dst_ref=part.at[2 + side],
            send_sem=part_send.at[side],
            recv_sem=part_recv.at[side],
            device_id={"brick": peer_of[side]},
            device_id_type=MESH,
        )

    for side in range(2):
        part[side] = to_coarse(ry[...], rz, X[2 * side])

    for side in range(2):

        @pl.when(has[side])
        def _():
            partial(side).start()

    own[...] = to_coarse(ry[...], rz, X[1])
    for side in range(2):

        @pl.when(has[side])
        def _():
            partial_in(side).wait_recv()
            own[...] = own[...] + part[2 + side]

    own[...] = own[...] * (1.0 / 64.0)
    stores[1].start()

    def send_r(k, _):
        spread(own, all_rhs, k, r_send, r_recv).start()
        return 0

    lax.fori_loop(1, n, send_r, 0)

    def settle_q(k, _):
        landed(all_q, k, q_send, q_recv).wait_recv()
        spread(all_q.at[me], all_q, k, q_send, q_recv).wait_send()
        return 0

    def settle_r(k, _):
        landed(all_rhs, k, r_send, r_recv).wait_recv()
        spread(own, all_rhs, k, r_send, r_recv).wait_send()
        return 0

    lax.fori_loop(1, n, settle_q, 0)
    coarse_coefficients(n, min(8, n), all_q, q_pad, coef, scaled)
    stores[2].start()
    stores[3].start()

    for side in range(2):

        @pl.when(has[side])
        def _():
            for c in range(CHUNKS):
                for which in range(3):
                    halo(which, side, c).wait_send()
            partial(side).wait_send()

    lax.fori_loop(1, n, settle_r, 0)
    for copy in stores:
        copy.wait()


def coarse_shifts(shape):
    rows, lanes = shape[1:]
    cz = lanes // 2
    row = lax.broadcasted_iota(jnp.int32, shape, 1)
    lane = lax.broadcasted_iota(jnp.int32, shape, 2)
    low_half = lane < cz
    z = jnp.where(low_half, lane, lane - cz)
    outside = (
        (row == 0) & low_half,
        (row == rows - 1) & jnp.logical_not(low_half),
        z == 0,
        z == cz - 1,
    )

    def shifts(c):
        swapped = pltpu.roll(c, cz, 2)
        y_low = jnp.where(low_half, pltpu.roll(swapped, 1, 1), swapped)
        y_high = jnp.where(low_half, swapped, pltpu.roll(swapped, rows - 1, 1))
        return y_low, y_high, pltpu.roll(c, 1, 2), pltpu.roll(c, lanes - 1, 2)

    return shifts, outside


def coarse_coefficients(n, group, perm, q_pad, coef, scaled):
    rows, lanes = perm.shape[1:]
    shifts, outside = coarse_shifts((group, rows, lanes))
    edge = jnp.zeros((rows, lanes), F32)
    q_pad[0] = edge
    q_pad[n + 1] = edge
    q_pad[1 : n + 1] = perm[...]

    def prepare(g, _):
        at = pl.multiple_of(g * group, group)
        q = q_pad[pl.ds(at + 1, group)]
        near = [q_pad[pl.ds(at, group)], q_pad[pl.ds(at + 2, group)]]
        near += [jnp.where(out, 0.0, v) for out, v in zip(outside, shifts(q))]
        faces = [0.5 * (q + v) for v in near]
        diagonal = ((faces[0] + faces[1]) + (faces[2] + faces[3])) + (faces[4] + faces[5])
        scale = 0.8 / diagonal
        for k, out in enumerate((None, None) + outside):
            f = faces[k] * scale
            coef[k, pl.ds(at, group)] = f if out is None else jnp.where(out, 0.0, f)
        scaled[pl.ds(at, group)] = 16.0 * scale
        return 0

    lax.fori_loop(0, n // group, prepare, 0)


def coarse_kernel(
    n, group,
    owner_hbm, rhs_hbm, coef_hbm, scaled_hbm, smooth_hbm, ez_hbm, ey_hbm,
    corrected_hbm, held,
    owner, rhs, coef, scaled, smooth, ez, ey, C, B, corrected, sem,
):
    me = lax.axis_index("brick")
    loads = [
        pltpu.make_async_copy(*pair, sem.at[4 + k])
        for k, pair in enumerate(
            (
                (rhs_hbm, rhs), (scaled_hbm, scaled), (coef_hbm, coef),
                (ez_hbm, ez), (ey_hbm, ey), (smooth_hbm, smooth), (owner_hbm, owner),
            )
        )
    ]
    for load in loads:
        load.start()
    rows, lanes = rhs.shape[1:]
    shifts, _ = coarse_shifts((group, rows, lanes))
    edge = jnp.zeros((rows, lanes), F32)
    for slot in range(2):
        C[slot, 0] = edge
        C[slot, n + 1] = edge
    loads[0].wait()
    loads[1].wait()
    B[...] = rhs[...] * scaled[...]
    C[0, 1 : n + 1] = B[...]

    loads[2].wait()
    for sweep in range(SWEEPS - 1):
        now, later = sweep % 2, 1 - sweep % 2

        def step(g, _):
            at = pl.multiple_of(g * group, group)
            c = C[now, pl.ds(at + 1, group)]
            near = (C[now, pl.ds(at, group)], C[now, pl.ds(at + 2, group)]) + shifts(c)
            terms = [coef[k, pl.ds(at, group)] * v for k, v in enumerate(near)]
            total = B[pl.ds(at, group)] + 0.2 * c
            total = (total + (terms[0] + terms[1])) + ((terms[2] + terms[3]) + (terms[4] + terms[5]))
            C[later, pl.ds(at + 1, group)] = total
            return 0

        lax.fori_loop(0, n // group, step, 0)

    final = (SWEEPS - 1) % 2

    for load in loads[3:]:
        load.wait()
    below, mid, above = C[final, me], C[final, me + 1], C[final, me + 2]
    planes = jnp.concatenate(
        [
            0.625 * mid + 0.375 * below,
            0.875 * mid + 0.125 * below,
            0.875 * mid + 0.125 * above,
            0.625 * mid + 0.375 * above,
        ],
        axis=0,
    )
    hi, lo = split(planes)
    even = dot(hi, ez[0]) + dot(lo, ez[0])
    odd = dot(hi, ez[1]) + dot(lo, ez[1])
    for p in range(4):
        both = jnp.concatenate(
            [even[p * rows : (p + 1) * rows], odd[p * rows : (p + 1) * rows]], axis=0
        )
        hi, lo = split(both)
        corrected[p] = smooth[p] + (dot(ey[...], hi) + dot(ey[...], lo))
        pltpu.make_async_copy(corrected.at[p], corrected_hbm.at[p], sem.at[p]).start()

    mine = jnp.zeros((rows, lanes), F32)
    for b in range(n):
        mine = jnp.where(owner[b] == me, C[final, b + 1], mine)
    for r in range(rows):
        held[0:1, r * lanes : (r + 1) * lanes] = mine[r : r + 1]
    for p in range(4):
        pltpu.make_async_copy(corrected.at[p], corrected_hbm.at[p], sem.at[p]).wait()


def local(n, source, guess, log_perm, owner):
    planes, ny, nz = source.shape
    assert planes == 4
    cells = (ny // 4) * (nz // 4)
    rows, lanes = ny // 8, nz // 2
    dense = (rows, lanes)
    as_bf16 = lambda m: jnp.asarray(m.astype(ml_dtypes.bfloat16))
    py, pz = even_odd(prolong_matrix(ny)), prolong_matrix(nz)
    ry, rz = as_bf16(py.T), as_bf16(halves(pz))
    my, mz = as_bf16(even_odd(mean_matrix(ny)).T), as_bf16(halves(mean_matrix(nz)))
    ey, ez = as_bf16(py), as_bf16(halves(pz).transpose(0, 2, 1))
    vmem = pl.BlockSpec(memory_space=pltpu.VMEM)
    hbm = pl.BlockSpec(memory_space=pl.ANY)
    whole = lambda *s: pltpu.VMEM(s, F32)
    dma = lambda *s: pltpu.SemaphoreType.DMA(s)
    padded = (6, ny + 16, nz)
    smooth, all_rhs, coef, scaled = pl.pallas_call(
        functools.partial(smooth_kernel, n, ny, nz),
        out_shape=(
            jax.ShapeDtypeStruct((4, ny, nz), F32),
            jax.ShapeDtypeStruct((n,) + dense, F32),
            jax.ShapeDtypeStruct((6, n) + dense, F32),
            jax.ShapeDtypeStruct((n,) + dense, F32),
        ),
        in_specs=[hbm] * 7,
        out_specs=(hbm,) * 4,
        scratch_shapes=[
            whole(6, n, *dense), whole(n, *dense),
            pltpu.VMEM(ry.shape, BF16), pltpu.VMEM(rz.shape, BF16),
            pltpu.VMEM(my.shape, BF16), pltpu.VMEM(mz.shape, BF16),
            whole(n, *dense), whole(n + 2, *dense),
            whole(4, ny, nz), whole(4, ny, nz),
            whole(*padded), whole(*padded), whole(*padded), whole(*padded),
            whole(4, ny, nz), whole(4, ny, nz),
            whole(2, ny, nz), whole(3, ny, nz), whole(3, 2, ny, nz),
            whole(*dense), whole(4, *dense),
            dma(7), dma(3, 2, CHUNKS), dma(3, 2, CHUNKS), dma(2), dma(2),
            dma(n), dma(n), dma(n), dma(n),
        ],
        compiler_params=pltpu.CompilerParams(
            collective_id=0, has_side_effects=True, vmem_limit_bytes=60 * 2**20
        ),
        name="smooth",
    )(source, guess, log_perm, ry, rz, my, mz)
    return pl.pallas_call(
        functools.partial(coarse_kernel, n, min(8, n)),
        out_shape=(
            jax.ShapeDtypeStruct((4, ny, nz), F32),
            jax.ShapeDtypeStruct((1, cells), F32),
        ),
        in_specs=[hbm] * 7,
        out_specs=(hbm, vmem),
        scratch_shapes=[
            pltpu.SMEM((n,), jnp.int32),
            whole(n, *dense), whole(6, n, *dense), whole(n, *dense), whole(4, ny, nz),
            pltpu.VMEM(ez.shape, BF16), pltpu.VMEM(ey.shape, BF16),
            whole(2, n + 2, *dense), whole(n, *dense), whole(4, ny, nz), dma(11),
        ],
        compiler_params=pltpu.CompilerParams(vmem_limit_bytes=60 * 2**20),
        name="coarse",
    )(owner, all_rhs, coef, scaled, smooth, ez, ey)


def solution(mesh):
    spec = P(("samples", "brick"), None, None)
    return jax.shard_map(
        functools.partial(local, mesh.shape["brick"]),
        mesh=mesh,
        in_specs=(spec, spec, spec, P()),
        out_specs=(spec, P(("samples", "brick"), None)),
        check_vma=False,
    )
```

```python
import functools

import jax
import jax.numpy as jnp
import ml_dtypes
import numpy as np
from jax import lax
from jax.experimental import pallas as pl
from jax.experimental.pallas import tpu as pltpu
from jax.sharding import PartitionSpec as P

SWEEPS = 8
CHUNKS = 8
MESH = pl.DeviceIdType.MESH
F32 = jnp.float32
BF16 = jnp.bfloat16


def prolong_matrix(n_fine):
    i = np.arange(n_fine)[:, None]
    j = np.arange(n_fine // 4)[None, :]
    base, offset = i // 4, i % 4
    own = np.where((offset == 0) | (offset == 3), 0.625, 0.875)
    side = np.where(offset < 2, -1, 1)
    return np.where(j == base, own, 0.0) + np.where(j == base + side, 1.0 - own, 0.0)


def mean_matrix(n_fine):
    i = np.arange(n_fine)[:, None]
    j = np.arange(n_fine // 4)[None, :]
    return np.where(j == i // 4, 1.0, 0.0)


def even_odd(m):
    return np.concatenate([m[:, 0::2], m[:, 1::2]], axis=1)


def halves(m):
    zero = np.zeros_like(m)
    return np.stack([np.concatenate([m, zero], 1), np.concatenate([zero, m], 1)])


def split(x):
    hi = x.astype(BF16)
    return hi, (x - hi.astype(F32)).astype(BF16)


def dot(a, b):
    return jnp.dot(a, b, preferred_element_type=F32)


def to_coarse(y_mat, z_mat, x):
    hi, lo = split(x)
    a = dot(y_mat, hi) + dot(y_mat, lo)
    hi, lo = split(a)
    h = a.shape[0] // 2
    return (
        dot(hi[:h], z_mat[0]) + dot(lo[:h], z_mat[0]) + dot(hi[h:], z_mat[1]) + dot(lo[h:], z_mat[1])
    )


def smooth_kernel(
    n, ny, nz,
    source_hbm, guess_hbm, logq_hbm, ry_hbm, rz_hbm, my_hbm, mz_hbm,
    smooth_hbm, all_rhs, coef_hbm, scaled_hbm,
    coef, scaled, ry, rz, my, mz, all_q, q_pad, src, logq, K, U0, U1, U2, D, N, EK, X, H, own, part,
    local_sem, halo_send, halo_recv, part_send, part_recv, q_send, q_recv, r_send, r_recv,
):
    me = lax.axis_index("brick")
    R = ny // CHUNKS
    has = (me > 0, me < n - 1)
    peer_of = (me - 1, me + 1)

    loads = [
        pltpu.make_async_copy(logq_hbm, logq, local_sem.at[0]),
        pltpu.make_async_copy(guess_hbm, U0.at[pl.ds(1, 4), pl.ds(8, ny)], local_sem.at[1]),
        pltpu.make_async_copy(source_hbm, src, local_sem.at[2]),
        pltpu.make_async_copy(my_hbm, my, local_sem.at[3]),
        pltpu.make_async_copy(mz_hbm, mz, local_sem.at[4]),
        pltpu.make_async_copy(ry_hbm, ry, local_sem.at[5]),
        pltpu.make_async_copy(rz_hbm, rz, local_sem.at[6]),
    ]
    for copy in loads:
        copy.start()

    barrier = pltpu.get_barrier_semaphore()

    def greet(k, _):
        pl.semaphore_signal(
            barrier, inc=1, device_id={"brick": lax.rem(me + k, n)}, device_id_type=MESH
        )
        return 0

    lax.fori_loop(1, n, greet, 0)
    pl.semaphore_wait(barrier, n - 1)

    def halo(which, side, c):
        plane = 3 * side
        start = c * R if isinstance(c, int) else pl.multiple_of(c * R, R)
        rows = pl.ds(start, R)
        if which == 2:
            ref = U1.at[plane + 1, pl.ds(start + 8, R)]
        else:
            ref = (logq_hbm, guess_hbm)[which].at[plane, rows]
        return pltpu.make_async_remote_copy(
            src_ref=ref,
            dst_ref=H.at[which, 1 - side, rows],
            send_sem=halo_send.at[which, side, c],
            recv_sem=halo_recv.at[which, 1 - side, c],
            device_id={"brick": peer_of[side]},
            device_id_type=MESH,
        )

    def arrival(which, side, c):
        start = c * R if isinstance(c, int) else pl.multiple_of(c * R, R)
        ref = H.at[which, side, pl.ds(start, R)]
        return pltpu.make_async_remote_copy(
            src_ref=ref,
            dst_ref=ref,
            send_sem=halo_send.at[which, side, c],
            recv_sem=halo_recv.at[which, side, c],
            device_id={"brick": peer_of[side]},
            device_id_type=MESH,
        )

    for c in range(CHUNKS):
        for side in range(2):

            @pl.when(has[side])
            def _():
                halo(0, side, c).start()
                halo(1, side, c).start()

    zero_plane = jnp.zeros((ny + 16, nz), F32)
    zero_rows = jnp.zeros((8, nz), F32)
    for ref in (K, U0, U1, U2):
        ref[0] = zero_plane
        ref[5] = zero_plane
        for p in range(1, 5):
            ref[p, 0:8] = zero_rows
            ref[p, ny + 8 : ny + 16] = zero_rows

    lane = lax.broadcasted_iota(jnp.int32, (R, nz), 1)
    first, last = lane == 0, lane == nz - 1

    def yz(window):
        center = window[8 : R + 8]
        low = jnp.where(first, 0.0, pltpu.roll(center, 1, 1))
        high = jnp.where(last, 0.0, pltpu.roll(center, nz - 1, 1))
        return (window[7 : R + 7] + window[9 : R + 9]) + (low + high)

    loads[0].wait()

    def exps(i, _):
        p, start = i // CHUNKS, pl.multiple_of((i % CHUNKS) * R, R)
        K[p + 1, pl.ds(start + 8, R)] = jnp.exp(logq[p, pl.ds(start, R)])
        return 0

    lax.fori_loop(0, 4 * CHUNKS, exps, 0)
    for copy in loads[1:]:
        copy.wait()

    def nearby(U, p, start):
        at = pl.ds(start + 8, R)
        window = pl.ds(start, R + 16)
        u, k = U[p + 1, window], K[p + 1, window]
        um, up, km, kp = U[p, at], U[p + 2, at], K[p, at], K[p + 2, at]
        su = yz(u) + (um + up)
        sku = yz(u * k) + (km * um + kp * up)
        q = k[8 : R + 8]
        return u[8 : R + 8], q, k, km + kp, 0.5 * (q * su + sku)

    def sweep_one(i, _):
        p, start = i // CHUNKS, pl.multiple_of((i % CHUNKS) * R, R)
        rows = pl.ds(start, R)
        u, q, k, kx, near = nearby(U0, p, start)
        d = 3.0 * q + 0.5 * (yz(k) + kx)
        total = src[p, rows] + near
        D[p, rows] = d
        N[p, rows] = total
        U1[p + 1, pl.ds(start + 8, R)] = 0.2 * u + 0.8 * total / d
        return 0

    lax.fori_loop(0, 4 * CHUNKS, sweep_one, 0)

    own[...] = to_coarse(
        my[...], mz, (K[1, 8 : ny + 8] + K[2, 8 : ny + 8]) + (K[3, 8 : ny + 8] + K[4, 8 : ny + 8])
    ) * (1.0 / 64.0)
    all_q[me] = own[...]

    def finish_one(c, _):
        start = pl.multiple_of(c * R, R)
        rows, at = pl.ds(start, R), pl.ds(start + 8, R)
        for side in range(2):
            p = 3 * side

            @pl.when(has[side])
            def _():
                arrival(0, side, c).wait_recv()
                arrival(1, side, c).wait_recv()
                q = K[p + 1, at]
                kh = jnp.exp(H[0, side, rows])
                EK[side, rows] = kh
                D[p, rows] = D[p, rows] + 0.5 * kh
                N[p, rows] = N[p, rows] + 0.5 * (q + kh) * H[1, side, rows]

            @pl.when(jnp.logical_not(has[side]))
            def _():
                EK[side, rows] = jnp.zeros((R, nz), F32)

            U1[p + 1, at] = 0.2 * U0[p + 1, at] + 0.8 * N[p, rows] / D[p, rows]

            @pl.when(has[side])
            def _():
                halo(2, side, c).start()

        return 0

    def spread(block, ref, k, send, recv):
        return pltpu.make_async_remote_copy(
            src_ref=block,
            dst_ref=ref.at[me],
            send_sem=send.at[k],
            recv_sem=recv.at[me],
            device_id={"brick": lax.rem(me + k, n)},
            device_id_type=MESH,
        )

    def landed(ref, k, send, recv):
        who = lax.rem(me + k, n)
        return pltpu.make_async_remote_copy(
            src_ref=ref.at[who],
            dst_ref=ref.at[who],
            send_sem=send.at[k],
            recv_sem=recv.at[who],
            device_id={"brick": who},
            device_id_type=MESH,
        )

    def send_q(k, _):
        spread(all_q.at[me], all_q, k, q_send, q_recv).start()
        return 0

    def sweep_two(p, start):
        rows = pl.ds(start, R)
        u, q, k, kx, near = nearby(U1, p, start)
        total = src[p, rows] + near
        N[p, rows] = total
        U2[p + 1, pl.ds(start + 8, R)] = 0.2 * u + 0.8 * total / D[p, rows]
        return 0

    def first_stage(c, _):
        @pl.when(c < CHUNKS)
        def _():
            finish_one(c, 0)

        @pl.when(c == CHUNKS - 1)
        def _():
            lax.fori_loop(1, n, send_q, 0)

        @pl.when(c > 0)
        def _():
            start = pl.multiple_of((c - 1) * R, R)
            lax.fori_loop(0, 4, lambda p, _: sweep_two(p, start), 0)

        return 0

    lax.fori_loop(0, CHUNKS + 1, first_stage, 0)

    def finish_two(c, _):
        start = pl.multiple_of(c * R, R)
        rows, at = pl.ds(start, R), pl.ds(start + 8, R)
        for side in range(2):
            p = 3 * side

            @pl.when(has[side])
            def _():
                arrival(2, side, c).wait_recv()
                total = N[p, rows] + 0.5 * (K[p + 1, at] + EK[side, rows]) * H[2, side, rows]
                U2[p + 1, at] = 0.2 * U1[p + 1, at] + 0.8 * total / D[p, rows]

        return 0

    present = [jnp.where(flag, 0.5, 0.0).astype(F32) for flag in has]

    def residual(c, _):
        start = pl.multiple_of(c * R, R)
        rows, at = pl.ds(start, R), pl.ds(start + 8, R)

        def row(p):
            u, q, k, kx, near = nearby(U2, p, start)
            return src[p, rows] - D[p, rows] * u + near

        r0, r1 = row(0), row(1)
        flo = present[0] * (K[1, at] + EK[0, rows]) * U2[1, at]
        X[0, rows] = 0.625 * flo + 0.375 * r0 + 0.125 * r1
        X[1, rows] = 0.375 * flo + 0.625 * r0 + 0.875 * r1
        r2, r3 = row(2), row(3)
        fhi = present[1] * (K[4, at] + EK[1, rows]) * U2[4, at]
        X[2, rows] = 0.625 * fhi + 0.375 * r3 + 0.125 * r2
        X[1, rows] = X[1, rows] + (0.375 * fhi + 0.625 * r3 + 0.875 * r2)
        return 0

    def second_stage(c, _):
        @pl.when(c < CHUNKS)
        def _():
            finish_two(c, 0)

        @pl.when(c > 0)
        def _():
            residual(c - 1, 0)

        return 0

    lax.fori_loop(0, CHUNKS + 1, second_stage, 0)

    stores = [
        pltpu.make_async_copy(U2.at[pl.ds(1, 4), pl.ds(8, ny)], smooth_hbm, local_sem.at[0]),
        pltpu.make_async_copy(own, all_rhs.at[me], local_sem.at[1]),
        pltpu.make_async_copy(coef, coef_hbm, local_sem.at[2]),
        pltpu.make_async_copy(scaled, scaled_hbm, local_sem.at[3]),
    ]
    stores[0].start()

    def partial(side):
        return pltpu.make_async_remote_copy(
            src_ref=part.at[side],
            dst_ref=part.at[3 - side],
            send_sem=part_send.at[side],
            recv_sem=part_recv.at[1 - side],
            device_id={"brick": peer_of[side]},
            device_id_type=MESH,
        )

    def partial_in(side):
        return pltpu.make_async_remote_copy(
            src_ref=part.at[2 + side],
            dst_ref=part.at[2 + side],
            send_sem=part_send.at[side],
            recv_sem=part_recv.at[side],
            device_id={"brick": peer_of[side]},
            device_id_type=MESH,
        )

    for side in range(2):
        part[side] = to_coarse(ry[...], rz, X[2 * side])

    for side in range(2):

        @pl.when(has[side])
        def _():
            partial(side).start()

    own[...] = to_coarse(ry[...], rz, X[1])
    for side in range(2):

        @pl.when(has[side])
        def _():
            partial_in(side).wait_recv()
            own[...] = own[...] + part[2 + side]

    own[...] = own[...] * (1.0 / 64.0)
    stores[1].start()

    def send_r(k, _):
        spread(own, all_rhs, k, r_send, r_recv).start()
        return 0

    lax.fori_loop(1, n, send_r, 0)

    def settle_q(k, _):
        landed(all_q, k, q_send, q_recv).wait_recv()
        spread(all_q.at[me], all_q, k, q_send, q_recv).wait_send()
        return 0

    def settle_r(k, _):
        landed(all_rhs, k, r_send, r_recv).wait_recv()
        spread(own, all_rhs, k, r_send, r_recv).wait_send()
        return 0

    lax.fori_loop(1, n, settle_q, 0)
    coarse_coefficients(n, min(8, n), all_q, q_pad, coef, scaled)
    stores[2].start()
    stores[3].start()

    for side in range(2):

        @pl.when(has[side])
        def _():
            for c in range(CHUNKS):
                for which in range(3):
                    halo(which, side, c).wait_send()
            partial(side).wait_send()

    lax.fori_loop(1, n, settle_r, 0)
    for copy in stores:
        copy.wait()


def coarse_shifts(shape):
    rows, lanes = shape[1:]
    cz = lanes // 2
    row = lax.broadcasted_iota(jnp.int32, shape, 1)
    lane = lax.broadcasted_iota(jnp.int32, shape, 2)
    low_half = lane < cz
    z = jnp.where(low_half, lane, lane - cz)
    outside = (
        (row == 0) & low_half,
        (row == rows - 1) & jnp.logical_not(low_half),
        z == 0,
        z == cz - 1,
    )

    def shifts(c):
        swapped = pltpu.roll(c, cz, 2)
        y_low = jnp.where(low_half, pltpu.roll(swapped, 1, 1), swapped)
        y_high = jnp.where(low_half, swapped, pltpu.roll(swapped, rows - 1, 1))
        return y_low, y_high, pltpu.roll(c, 1, 2), pltpu.roll(c, lanes - 1, 2)

    return shifts, outside


def coarse_coefficients(n, group, perm, q_pad, coef, scaled):
    rows, lanes = perm.shape[1:]
    shifts, outside = coarse_shifts((group, rows, lanes))
    edge = jnp.zeros((rows, lanes), F32)
    q_pad[0] = edge
    q_pad[n + 1] = edge
    q_pad[1 : n + 1] = perm[...]

    def prepare(g, _):
        at = pl.multiple_of(g * group, group)
        q = q_pad[pl.ds(at + 1, group)]
        near = [q_pad[pl.ds(at, group)], q_pad[pl.ds(at + 2, group)]]
        near += [jnp.where(out, 0.0, v) for out, v in zip(outside, shifts(q))]
        faces = [0.5 * (q + v) for v in near]
        diagonal = ((faces[0] + faces[1]) + (faces[2] + faces[3])) + (faces[4] + faces[5])
        scale = 0.8 / diagonal
        for k, out in enumerate((None, None) + outside):
            f = faces[k] * scale
            coef[k, pl.ds(at, group)] = f if out is None else jnp.where(out, 0.0, f)
        scaled[pl.ds(at, group)] = 16.0 * scale
        return 0

    lax.fori_loop(0, n // group, prepare, 0)


def coarse_kernel(
    n, group,
    owner_hbm, rhs_hbm, coef_hbm, scaled_hbm, smooth_hbm, ez_hbm, ey_hbm,
    corrected_hbm, held,
    owner, rhs, coef, scaled, smooth, ez, ey, C, B, corrected, sem,
):
    me = lax.axis_index("brick")
    loads = [
        pltpu.make_async_copy(*pair, sem.at[4 + k])
        for k, pair in enumerate(
            (
                (rhs_hbm, rhs), (scaled_hbm, scaled), (coef_hbm, coef),
                (ez_hbm, ez), (ey_hbm, ey), (smooth_hbm, smooth), (owner_hbm, owner),
            )
        )
    ]
    for load in loads:
        load.start()
    rows, lanes = rhs.shape[1:]
    shifts, _ = coarse_shifts((group, rows, lanes))
    edge = jnp.zeros((rows, lanes), F32)
    for slot in range(2):
        C[slot, 0] = edge
        C[slot, n + 1] = edge
    loads[0].wait()
    loads[1].wait()
    B[...] = rhs[...] * scaled[...]
    C[0, 1 : n + 1] = B[...]

    loads[2].wait()
    for sweep in range(SWEEPS - 1):
        now, later = sweep % 2, 1 - sweep % 2

        def step(g, _):
            at = pl.multiple_of(g * group, group)
            c = C[now, pl.ds(at + 1, group)]
            near = (C[now, pl.ds(at, group)], C[now, pl.ds(at + 2, group)]) + shifts(c)
            terms = [coef[k, pl.ds(at, group)] * v for k, v in enumerate(near)]
            total = B[pl.ds(at, group)] + 0.2 * c
            total = (total + (terms[0] + terms[1])) + ((terms[2] + terms[3]) + (terms[4] + terms[5]))
            C[later, pl.ds(at + 1, group)] = total
            return 0

        lax.fori_loop(0, n // group, step, 0)

    final = (SWEEPS - 1) % 2

    for load in loads[3:]:
        load.wait()
    below, mid, above = C[final, me], C[final, me + 1], C[final, me + 2]
    planes = jnp.concatenate(
        [
            0.625 * mid + 0.375 * below,
            0.875 * mid + 0.125 * below,
            0.875 * mid + 0.125 * above,
            0.625 * mid + 0.375 * above,
        ],
        axis=0,
    )
    hi, lo = split(planes)
    even = dot(hi, ez[0]) + dot(lo, ez[0])
    odd = dot(hi, ez[1]) + dot(lo, ez[1])
    for p in range(4):
        both = jnp.concatenate(
            [even[p * rows : (p + 1) * rows], odd[p * rows : (p + 1) * rows]], axis=0
        )
        hi, lo = split(both)
        corrected[p] = smooth[p] + (dot(ey[...], hi) + dot(ey[...], lo))
        pltpu.make_async_copy(corrected.at[p], corrected_hbm.at[p], sem.at[p]).start()

    mine = jnp.zeros((rows, lanes), F32)
    for b in range(n):
        mine = jnp.where(owner[b] == me, C[final, b + 1], mine)
    for r in range(rows):
        held[0:1, r * lanes : (r + 1) * lanes] = mine[r : r + 1]
    for p in range(4):
        pltpu.make_async_copy(corrected.at[p], corrected_hbm.at[p], sem.at[p]).wait()


def local(n, source, guess, log_perm, owner):
    planes, ny, nz = source.shape
    assert planes == 4
    cells = (ny // 4) * (nz // 4)
    rows, lanes = ny // 8, nz // 2
    dense = (rows, lanes)
    as_bf16 = lambda m: jnp.asarray(m.astype(ml_dtypes.bfloat16))
    py, pz = even_odd(prolong_matrix(ny)), prolong_matrix(nz)
    ry, rz = as_bf16(py.T), as_bf16(halves(pz))
    my, mz = as_bf16(even_odd(mean_matrix(ny)).T), as_bf16(halves(mean_matrix(nz)))
    ey, ez = as_bf16(py), as_bf16(halves(pz).transpose(0, 2, 1))
    vmem = pl.BlockSpec(memory_space=pltpu.VMEM)
    hbm = pl.BlockSpec(memory_space=pl.ANY)
    whole = lambda *s: pltpu.VMEM(s, F32)
    dma = lambda *s: pltpu.SemaphoreType.DMA(s)
    padded = (6, ny + 16, nz)
    smooth, all_rhs, coef, scaled = pl.pallas_call(
        functools.partial(smooth_kernel, n, ny, nz),
        out_shape=(
            jax.ShapeDtypeStruct((4, ny, nz), F32),
            jax.ShapeDtypeStruct((n,) + dense, F32),
            jax.ShapeDtypeStruct((6, n) + dense, F32),
            jax.ShapeDtypeStruct((n,) + dense, F32),
        ),
        in_specs=[hbm] * 7,
        out_specs=(hbm,) * 4,
        scratch_shapes=[
            whole(6, n, *dense), whole(n, *dense),
            pltpu.VMEM(ry.shape, BF16), pltpu.VMEM(rz.shape, BF16),
            pltpu.VMEM(my.shape, BF16), pltpu.VMEM(mz.shape, BF16),
            whole(n, *dense), whole(n + 2, *dense),
            whole(4, ny, nz), whole(4, ny, nz),
            whole(*padded), whole(*padded), whole(*padded), whole(*padded),
            whole(4, ny, nz), whole(4, ny, nz),
            whole(2, ny, nz), whole(3, ny, nz), whole(3, 2, ny, nz),
            whole(*dense), whole(4, *dense),
            dma(7), dma(3, 2, CHUNKS), dma(3, 2, CHUNKS), dma(2), dma(2),
            dma(n), dma(n), dma(n), dma(n),
        ],
        compiler_params=pltpu.CompilerParams(
            collective_id=0, has_side_effects=True, vmem_limit_bytes=60 * 2**20
        ),
        name="smooth",
    )(source, guess, log_perm, ry, rz, my, mz)
    return pl.pallas_call(
        functools.partial(coarse_kernel, n, min(8, n)),
        out_shape=(
            jax.ShapeDtypeStruct((4, ny, nz), F32),
            jax.ShapeDtypeStruct((1, cells), F32),
        ),
        in_specs=[hbm] * 7,
        out_specs=(hbm, vmem),
        scratch_shapes=[
            pltpu.SMEM((n,), jnp.int32),
            whole(n, *dense), whole(6, n, *dense), whole(n, *dense), whole(4, ny, nz),
            pltpu.VMEM(ez.shape, BF16), pltpu.VMEM(ey.shape, BF16),
            whole(2, n + 2, *dense), whole(n, *dense), whole(4, ny, nz), dma(11),
        ],
        compiler_params=pltpu.CompilerParams(vmem_limit_bytes=60 * 2**20),
        name="coarse",
    )(owner, all_rhs, coef, scaled, smooth, ez, ey)


def solution(mesh):
    spec = P(("samples", "brick"), None, None)
    return jax.shard_map(
        functools.partial(local, mesh.shape["brick"]),
        mesh=mesh,
        in_specs=(spec, spec, spec, P()),
        out_specs=(spec, P(("samples", "brick"), None)),
        check_vma=False,
    )
```

```python
import functools

import jax
import jax.numpy as jnp
import ml_dtypes
import numpy as np
from jax import lax
from jax.experimental import pallas as pl
from jax.experimental.pallas import tpu as pltpu
from jax.sharding import PartitionSpec as P

SWEEPS = 8
CHUNKS = 8
MESH = pl.DeviceIdType.MESH
F32 = jnp.float32
BF16 = jnp.bfloat16


def prolong_matrix(n_fine):
    i = np.arange(n_fine)[:, None]
    j = np.arange(n_fine // 4)[None, :]
    base, offset = i // 4, i % 4
    own = np.where((offset == 0) | (offset == 3), 0.625, 0.875)
    side = np.where(offset < 2, -1, 1)
    return np.where(j == base, own, 0.0) + np.where(j == base + side, 1.0 - own, 0.0)


def mean_matrix(n_fine):
    i = np.arange(n_fine)[:, None]
    j = np.arange(n_fine // 4)[None, :]
    return np.where(j == i // 4, 1.0, 0.0)


def even_odd(m):
    return np.concatenate([m[:, 0::2], m[:, 1::2]], axis=1)


def halves(m):
    zero = np.zeros_like(m)
    return np.stack([np.concatenate([m, zero], 1), np.concatenate([zero, m], 1)])


def split(x):
    hi = x.astype(BF16)
    return hi, (x - hi.astype(F32)).astype(BF16)


def dot(a, b):
    return jnp.dot(a, b, preferred_element_type=F32)


def to_coarse(y_mat, z_mat, x):
    hi, lo = split(x)
    a = dot(y_mat, hi) + dot(y_mat, lo)
    hi, lo = split(a)
    h = a.shape[0] // 2
    return (
        dot(hi[:h], z_mat[0]) + dot(lo[:h], z_mat[0]) + dot(hi[h:], z_mat[1]) + dot(lo[h:], z_mat[1])
    )


def smooth_kernel(
    n, ny, nz,
    source_hbm, guess_hbm, logq_hbm, ry_hbm, rz_hbm, my_hbm, mz_hbm,
    smooth_hbm, all_rhs, coef_hbm, scaled_hbm,
    coef, scaled, ry, rz, my, mz, all_q, q_pad, src, logq, K, U0, U1, U2, D, N, EK, X, H, own, part,
    local_sem, halo_send, halo_recv, part_send, part_recv, q_send, q_recv, r_send, r_recv,
):
    me = lax.axis_index("brick")
    R = ny // CHUNKS
    has = (me > 0, me < n - 1)
    peer_of = (me - 1, me + 1)

    loads = [
        pltpu.make_async_copy(logq_hbm, logq, local_sem.at[0]),
        pltpu.make_async_copy(guess_hbm, U0.at[pl.ds(1, 4), pl.ds(8, ny)], local_sem.at[1]),
        pltpu.make_async_copy(source_hbm, src, local_sem.at[2]),
        pltpu.make_async_copy(my_hbm, my, local_sem.at[3]),
        pltpu.make_async_copy(mz_hbm, mz, local_sem.at[4]),
        pltpu.make_async_copy(ry_hbm, ry, local_sem.at[5]),
        pltpu.make_async_copy(rz_hbm, rz, local_sem.at[6]),
    ]
    for copy in loads:
        copy.start()

    barrier = pltpu.get_barrier_semaphore()

    def greet(k, _):
        pl.semaphore_signal(
            barrier, inc=1, device_id={"brick": lax.rem(me + k, n)}, device_id_type=MESH
        )
        return 0

    lax.fori_loop(1, n, greet, 0)
    pl.semaphore_wait(barrier, n - 1)

    def halo(which, side, c):
        plane = 3 * side
        start = c * R if isinstance(c, int) else pl.multiple_of(c * R, R)
        rows = pl.ds(start, R)
        if which == 2:
            ref = U1.at[plane + 1, pl.ds(start + 8, R)]
        else:
            ref = (logq_hbm, guess_hbm)[which].at[plane, rows]
        return pltpu.make_async_remote_copy(
            src_ref=ref,
            dst_ref=H.at[which, 1 - side, rows],
            send_sem=halo_send.at[which, side, c],
            recv_sem=halo_recv.at[which, 1 - side, c],
            device_id={"brick": peer_of[side]},
            device_id_type=MESH,
        )

    def arrival(which, side, c):
        start = c * R if isinstance(c, int) else pl.multiple_of(c * R, R)
        ref = H.at[which, side, pl.ds(start, R)]
        return pltpu.make_async_remote_copy(
            src_ref=ref,
            dst_ref=ref,
            send_sem=halo_send.at[which, side, c],
            recv_sem=halo_recv.at[which, side, c],
            device_id={"brick": peer_of[side]},
            device_id_type=MESH,
        )

    for c in range(CHUNKS):
        for side in range(2):

            @pl.when(has[side])
            def _():
                halo(0, side, c).start()
                halo(1, side, c).start()

    zero_plane = jnp.zeros((ny + 16, nz), F32)
    zero_rows = jnp.zeros((8, nz), F32)
    for ref in (K, U0, U1, U2):
        ref[0] = zero_plane
        ref[5] = zero_plane
        for p in range(1, 5):
            ref[p, 0:8] = zero_rows
            ref[p, ny + 8 : ny + 16] = zero_rows

    lane = lax.broadcasted_iota(jnp.int32, (R, nz), 1)
    first, last = lane == 0, lane == nz - 1

    def yz(window):
        center = window[8 : R + 8]
        low = jnp.where(first, 0.0, pltpu.roll(center, 1, 1))
        high = jnp.where(last, 0.0, pltpu.roll(center, nz - 1, 1))
        return (window[7 : R + 7] + window[9 : R + 9]) + (low + high)

    loads[0].wait()

    def exps(i, _):
        p, start = i // CHUNKS, pl.multiple_of((i % CHUNKS) * R, R)
        K[p + 1, pl.ds(start + 8, R)] = jnp.exp(logq[p, pl.ds(start, R)])
        return 0

    lax.fori_loop(0, 4 * CHUNKS, exps, 0)
    for copy in loads[1:]:
        copy.wait()

    def nearby(U, p, start):
        at = pl.ds(start + 8, R)
        window = pl.ds(start, R + 16)
        u, k = U[p + 1, window], K[p + 1, window]
        um, up, km, kp = U[p, at], U[p + 2, at], K[p, at], K[p + 2, at]
        su = yz(u) + (um + up)
        sku = yz(u * k) + (km * um + kp * up)
        q = k[8 : R + 8]
        return u[8 : R + 8], q, k, km + kp, 0.5 * (q * su + sku)

    def sweep_one(i, _):
        p, start = i // CHUNKS, pl.multiple_of((i % CHUNKS) * R, R)
        rows = pl.ds(start, R)
        u, q, k, kx, near = nearby(U0, p, start)
        d = 3.0 * q + 0.5 * (yz(k) + kx)
        total = src[p, rows] + near
        D[p, rows] = d
        N[p, rows] = total
        U1[p + 1, pl.ds(start + 8, R)] = 0.2 * u + 0.8 * total / d
        return 0

    lax.fori_loop(0, 4 * CHUNKS, sweep_one, 0)

    own[...] = to_coarse(
        my[...], mz, (K[1, 8 : ny + 8] + K[2, 8 : ny + 8]) + (K[3, 8 : ny + 8] + K[4, 8 : ny + 8])
    ) * (1.0 / 64.0)
    all_q[me] = own[...]

    def finish_one(c, _):
        start = pl.multiple_of(c * R, R)
        rows, at = pl.ds(start, R), pl.ds(start + 8, R)
        for side in range(2):
            p = 3 * side

            @pl.when(has[side])
            def _():
                arrival(0, side, c).wait_recv()
                arrival(1, side, c).wait_recv()
                q = K[p + 1, at]
                kh = jnp.exp(H[0, side, rows])
                EK[side, rows] = kh
                D[p, rows] = D[p, rows] + 0.5 * kh
                N[p, rows] = N[p, rows] + 0.5 * (q + kh) * H[1, side, rows]

            @pl.when(jnp.logical_not(has[side]))
            def _():
                EK[side, rows] = jnp.zeros((R, nz), F32)

            U1[p + 1, at] = 0.2 * U0[p + 1, at] + 0.8 * N[p, rows] / D[p, rows]

            @pl.when(has[side])
            def _():
                halo(2, side, c).start()

        return 0

    def spread(block, ref, k, send, recv):
        return pltpu.make_async_remote_copy(
            src_ref=block,
            dst_ref=ref.at[me],
            send_sem=send.at[k],
            recv_sem=recv.at[me],
            device_id={"brick": lax.rem(me + k, n)},
            device_id_type=MESH,
        )

    def landed(ref, k, send, recv):
        who = lax.rem(me + k, n)
        return pltpu.make_async_remote_copy(
            src_ref=ref.at[who],
            dst_ref=ref.at[who],
            send_sem=send.at[k],
            recv_sem=recv.at[who],
            device_id={"brick": who},
            device_id_type=MESH,
        )

    def send_q(k, _):
        spread(all_q.at[me], all_q, k, q_send, q_recv).start()
        return 0

    def sweep_two(p, start):
        rows = pl.ds(start, R)
        u, q, k, kx, near = nearby(U1, p, start)
        total = src[p, rows] + near
        N[p, rows] = total
        U2[p + 1, pl.ds(start + 8, R)] = 0.2 * u + 0.8 * total / D[p, rows]
        return 0

    def first_stage(c, _):
        @pl.when(c < CHUNKS)
        def _():
            finish_one(c, 0)

        @pl.when(c == CHUNKS - 1)
        def _():
            lax.fori_loop(1, n, send_q, 0)

        @pl.when(c > 0)
        def _():
            start = pl.multiple_of((c - 1) * R, R)
            lax.fori_loop(0, 4, lambda p, _: sweep_two(p, start), 0)

        return 0

    lax.fori_loop(0, CHUNKS + 1, first_stage, 0)

    def finish_two(c, _):
        start = pl.multiple_of(c * R, R)
        rows, at = pl.ds(start, R), pl.ds(start + 8, R)
        for side in range(2):
            p = 3 * side

            @pl.when(has[side])
            def _():
                arrival(2, side, c).wait_recv()
                total = N[p, rows] + 0.5 * (K[p + 1, at] + EK[side, rows]) * H[2, side, rows]
                U2[p + 1, at] = 0.2 * U1[p + 1, at] + 0.8 * total / D[p, rows]

        return 0

    present = [jnp.where(flag, 0.5, 0.0).astype(F32) for flag in has]

    def residual(c, _):
        start = pl.multiple_of(c * R, R)
        rows, at = pl.ds(start, R), pl.ds(start + 8, R)

        def row(p):
            u, q, k, kx, near = nearby(U2, p, start)
            return src[p, rows] - D[p, rows] * u + near

        r0, r1 = row(0), row(1)
        flo = present[0] * (K[1, at] + EK[0, rows]) * U2[1, at]
        X[0, rows] = 0.625 * flo + 0.375 * r0 + 0.125 * r1
        X[1, rows] = 0.375 * flo + 0.625 * r0 + 0.875 * r1
        r2, r3 = row(2), row(3)
        fhi = present[1] * (K[4, at] + EK[1, rows]) * U2[4, at]
        X[2, rows] = 0.625 * fhi + 0.375 * r3 + 0.125 * r2
        X[1, rows] = X[1, rows] + (0.375 * fhi + 0.625 * r3 + 0.875 * r2)
        return 0

    def second_stage(c, _):
        @pl.when(c < CHUNKS)
        def _():
            finish_two(c, 0)

        @pl.when(c > 0)
        def _():
            residual(c - 1, 0)

        return 0

    lax.fori_loop(0, CHUNKS + 1, second_stage, 0)

    stores = [
        pltpu.make_async_copy(U2.at[pl.ds(1, 4), pl.ds(8, ny)], smooth_hbm, local_sem.at[0]),
        pltpu.make_async_copy(own, all_rhs.at[me], local_sem.at[1]),
        pltpu.make_async_copy(coef, coef_hbm, local_sem.at[2]),
        pltpu.make_async_copy(scaled, scaled_hbm, local_sem.at[3]),
    ]
    stores[0].start()

    def partial(side):
        return pltpu.make_async_remote_copy(
            src_ref=part.at[side],
            dst_ref=part.at[3 - side],
            send_sem=part_send.at[side],
            recv_sem=part_recv.at[1 - side],
            device_id={"brick": peer_of[side]},
            device_id_type=MESH,
        )

    def partial_in(side):
        return pltpu.make_async_remote_copy(
            src_ref=part.at[2 + side],
            dst_ref=part.at[2 + side],
            send_sem=part_send.at[side],
            recv_sem=part_recv.at[side],
            device_id={"brick": peer_of[side]},
            device_id_type=MESH,
        )

    for side in range(2):
        part[side] = to_coarse(ry[...], rz, X[2 * side])

    for side in range(2):

        @pl.when(has[side])
        def _():
            partial(side).start()

    own[...] = to_coarse(ry[...], rz, X[1])
    for side in range(2):

        @pl.when(has[side])
        def _():
            partial_in(side).wait_recv()
            own[...] = own[...] + part[2 + side]

    own[...] = own[...] * (1.0 / 64.0)
    stores[1].start()

    def send_r(k, _):
        spread(own, all_rhs, k, r_send, r_recv).start()
        return 0

    lax.fori_loop(1, n, send_r, 0)

    def settle_q(k, _):
        landed(all_q, k, q_send, q_recv).wait_recv()
        spread(all_q.at[me], all_q, k, q_send, q_recv).wait_send()
        return 0

    def settle_r(k, _):
        landed(all_rhs, k, r_send, r_recv).wait_recv()
        spread(own, all_rhs, k, r_send, r_recv).wait_send()
        return 0

    lax.fori_loop(1, n, settle_q, 0)
    coarse_coefficients(n, min(8, n), all_q, q_pad, coef, scaled)
    stores[2].start()
    stores[3].start()

    for side in range(2):

        @pl.when(has[side])
        def _():
            for c in range(CHUNKS):
                for which in range(3):
                    halo(which, side, c).wait_send()
            partial(side).wait_send()

    lax.fori_loop(1, n, settle_r, 0)
    for copy in stores:
        copy.wait()


def coarse_shifts(shape):
    rows, lanes = shape[1:]
    cz = lanes // 2
    row = lax.broadcasted_iota(jnp.int32, shape, 1)
    lane = lax.broadcasted_iota(jnp.int32, shape, 2)
    low_half = lane < cz
    z = jnp.where(low_half, lane, lane - cz)
    outside = (
        (row == 0) & low_half,
        (row == rows - 1) & jnp.logical_not(low_half),
        z == 0,
        z == cz - 1,
    )

    def shifts(c):
        swapped = pltpu.roll(c, cz, 2)
        y_low = jnp.where(low_half, pltpu.roll(swapped, 1, 1), swapped)
        y_high = jnp.where(low_half, swapped, pltpu.roll(swapped, rows - 1, 1))
        return y_low, y_high, pltpu.roll(c, 1, 2), pltpu.roll(c, lanes - 1, 2)

    return shifts, outside


def coarse_coefficients(n, group, perm, q_pad, coef, scaled):
    rows, lanes = perm.shape[1:]
    shifts, outside = coarse_shifts((group, rows, lanes))
    edge = jnp.zeros((rows, lanes), F32)
    q_pad[0] = edge
    q_pad[n + 1] = edge
    q_pad[1 : n + 1] = perm[...]

    def prepare(g, _):
        at = pl.multiple_of(g * group, group)
        q = q_pad[pl.ds(at + 1, group)]
        near = [q_pad[pl.ds(at, group)], q_pad[pl.ds(at + 2, group)]]
        near += [jnp.where(out, 0.0, v) for out, v in zip(outside, shifts(q))]
        faces = [0.5 * (q + v) for v in near]
        diagonal = ((faces[0] + faces[1]) + (faces[2] + faces[3])) + (faces[4] + faces[5])
        scale = 0.8 / diagonal
        for k, out in enumerate((None, None) + outside):
            f = faces[k] * scale
            coef[k, pl.ds(at, group)] = f if out is None else jnp.where(out, 0.0, f)
        scaled[pl.ds(at, group)] = 16.0 * scale
        return 0

    lax.fori_loop(0, n // group, prepare, 0)


def coarse_kernel(
    n, group,
    owner_hbm, rhs_hbm, coef_hbm, scaled_hbm, smooth_hbm, ez_hbm, ey_hbm,
    corrected_hbm, held,
    owner, rhs, coef, scaled, smooth, ez, ey, C, B, corrected, sem,
):
    me = lax.axis_index("brick")
    loads = [
        pltpu.make_async_copy(*pair, sem.at[4 + k])
        for k, pair in enumerate(
            (
                (rhs_hbm, rhs), (scaled_hbm, scaled), (coef_hbm, coef),
                (ez_hbm, ez), (ey_hbm, ey), (smooth_hbm, smooth), (owner_hbm, owner),
            )
        )
    ]
    for load in loads:
        load.start()
    rows, lanes = rhs.shape[1:]
    shifts, _ = coarse_shifts((group, rows, lanes))
    edge = jnp.zeros((rows, lanes), F32)
    for slot in range(2):
        C[slot, 0] = edge
        C[slot, n + 1] = edge
    loads[0].wait()
    loads[1].wait()
    B[...] = rhs[...] * scaled[...]
    C[0, 1 : n + 1] = B[...]

    loads[2].wait()
    for sweep in range(SWEEPS - 1):
        now, later = sweep % 2, 1 - sweep % 2

        def step(g, _):
            at = pl.multiple_of(g * group, group)
            c = C[now, pl.ds(at + 1, group)]
            near = (C[now, pl.ds(at, group)], C[now, pl.ds(at + 2, group)]) + shifts(c)
            terms = [coef[k, pl.ds(at, group)] * v for k, v in enumerate(near)]
            total = B[pl.ds(at, group)] + 0.2 * c
            total = (total + (terms[0] + terms[1])) + ((terms[2] + terms[3]) + (terms[4] + terms[5]))
            C[later, pl.ds(at + 1, group)] = total
            return 0

        lax.fori_loop(0, n // group, step, 0)

    final = (SWEEPS - 1) % 2

    for load in loads[3:]:
        load.wait()
    below, mid, above = C[final, me], C[final, me + 1], C[final, me + 2]
    planes = jnp.concatenate(
        [
            0.625 * mid + 0.375 * below,
            0.875 * mid + 0.125 * below,
            0.875 * mid + 0.125 * above,
            0.625 * mid + 0.375 * above,
        ],
        axis=0,
    )
    hi, lo = split(planes)
    even = dot(hi, ez[0]) + dot(lo, ez[0])
    odd = dot(hi, ez[1]) + dot(lo, ez[1])
    for p in range(4):
        both = jnp.concatenate(
            [even[p * rows : (p + 1) * rows], odd[p * rows : (p + 1) * rows]], axis=0
        )
        hi, lo = split(both)
        corrected[p] = smooth[p] + (dot(ey[...], hi) + dot(ey[...], lo))
        pltpu.make_async_copy(corrected.at[p], corrected_hbm.at[p], sem.at[p]).start()

    mine = jnp.zeros((rows, lanes), F32)
    for b in range(n):
        mine = jnp.where(owner[b] == me, C[final, b + 1], mine)
    for r in range(rows):
        held[0:1, r * lanes : (r + 1) * lanes] = mine[r : r + 1]
    for p in range(4):
        pltpu.make_async_copy(corrected.at[p], corrected_hbm.at[p], sem.at[p]).wait()


def local(n, source, guess, log_perm, owner):
    planes, ny, nz = source.shape
    assert planes == 4
    cells = (ny // 4) * (nz // 4)
    rows, lanes = ny // 8, nz // 2
    dense = (rows, lanes)
    as_bf16 = lambda m: jnp.asarray(m.astype(ml_dtypes.bfloat16))
    py, pz = even_odd(prolong_matrix(ny)), prolong_matrix(nz)
    ry, rz = as_bf16(py.T), as_bf16(halves(pz))
    my, mz = as_bf16(even_odd(mean_matrix(ny)).T), as_bf16(halves(mean_matrix(nz)))
    ey, ez = as_bf16(py), as_bf16(halves(pz).transpose(0, 2, 1))
    vmem = pl.BlockSpec(memory_space=pltpu.VMEM)
    hbm = pl.BlockSpec(memory_space=pl.ANY)
    whole = lambda *s: pltpu.VMEM(s, F32)
    dma = lambda *s: pltpu.SemaphoreType.DMA(s)
    padded = (6, ny + 16, nz)
    smooth, all_rhs, coef, scaled = pl.pallas_call(
        functools.partial(smooth_kernel, n, ny, nz),
        out_shape=(
            jax.ShapeDtypeStruct((4, ny, nz), F32),
            jax.ShapeDtypeStruct((n,) + dense, F32),
            jax.ShapeDtypeStruct((6, n) + dense, F32),
            jax.ShapeDtypeStruct((n,) + dense, F32),
        ),
        in_specs=[hbm] * 7,
        out_specs=(hbm,) * 4,
        scratch_shapes=[
            whole(6, n, *dense), whole(n, *dense),
            pltpu.VMEM(ry.shape, BF16), pltpu.VMEM(rz.shape, BF16),
            pltpu.VMEM(my.shape, BF16), pltpu.VMEM(mz.shape, BF16),
            whole(n, *dense), whole(n + 2, *dense),
            whole(4, ny, nz), whole(4, ny, nz),
            whole(*padded), whole(*padded), whole(*padded), whole(*padded),
            whole(4, ny, nz), whole(4, ny, nz),
            whole(2, ny, nz), whole(3, ny, nz), whole(3, 2, ny, nz),
            whole(*dense), whole(4, *dense),
            dma(7), dma(3, 2, CHUNKS), dma(3, 2, CHUNKS), dma(2), dma(2),
            dma(n), dma(n), dma(n), dma(n),
        ],
        compiler_params=pltpu.CompilerParams(
            collective_id=0, has_side_effects=True, vmem_limit_bytes=60 * 2**20
        ),
        name="smooth",
    )(source, guess, log_perm, ry, rz, my, mz)
    return pl.pallas_call(
        functools.partial(coarse_kernel, n, min(16, n)),
        out_shape=(
            jax.ShapeDtypeStruct((4, ny, nz), F32),
            jax.ShapeDtypeStruct((1, cells), F32),
        ),
        in_specs=[hbm] * 7,
        out_specs=(hbm, vmem),
        scratch_shapes=[
            pltpu.SMEM((n,), jnp.int32),
            whole(n, *dense), whole(6, n, *dense), whole(n, *dense), whole(4, ny, nz),
            pltpu.VMEM(ez.shape, BF16), pltpu.VMEM(ey.shape, BF16),
            whole(2, n + 2, *dense), whole(n, *dense), whole(4, ny, nz), dma(11),
        ],
        compiler_params=pltpu.CompilerParams(vmem_limit_bytes=60 * 2**20),
        name="coarse",
    )(owner, all_rhs, coef, scaled, smooth, ez, ey)


def solution(mesh):
    spec = P(("samples", "brick"), None, None)
    return jax.shard_map(
        functools.partial(local, mesh.shape["brick"]),
        mesh=mesh,
        in_specs=(spec, spec, spec, P()),
        out_specs=(spec, P(("samples", "brick"), None)),
        check_vma=False,
    )
```

```python
import functools

import jax
import jax.numpy as jnp
import ml_dtypes
import numpy as np
from jax import lax
from jax.experimental import pallas as pl
from jax.experimental.pallas import tpu as pltpu
from jax.sharding import PartitionSpec as P

SWEEPS = 8
CHUNKS = 8
MESH = pl.DeviceIdType.MESH
F32 = jnp.float32
BF16 = jnp.bfloat16


def prolong_matrix(n_fine):
    i = np.arange(n_fine)[:, None]
    j = np.arange(n_fine // 4)[None, :]
    base, offset = i // 4, i % 4
    own = np.where((offset == 0) | (offset == 3), 0.625, 0.875)
    side = np.where(offset < 2, -1, 1)
    return np.where(j == base, own, 0.0) + np.where(j == base + side, 1.0 - own, 0.0)


def mean_matrix(n_fine):
    i = np.arange(n_fine)[:, None]
    j = np.arange(n_fine // 4)[None, :]
    return np.where(j == i // 4, 1.0, 0.0)


def even_odd(m):
    return np.concatenate([m[:, 0::2], m[:, 1::2]], axis=1)


def halves(m):
    zero = np.zeros_like(m)
    return np.stack([np.concatenate([m, zero], 1), np.concatenate([zero, m], 1)])


def split(x):
    hi = x.astype(BF16)
    return hi, (x - hi.astype(F32)).astype(BF16)


def dot(a, b):
    return jnp.dot(a, b, preferred_element_type=F32)


def to_coarse(y_mat, z_mat, x):
    hi, lo = split(x)
    a = dot(y_mat, hi) + dot(y_mat, lo)
    hi, lo = split(a)
    h = a.shape[0] // 2
    return (
        dot(hi[:h], z_mat[0]) + dot(lo[:h], z_mat[0]) + dot(hi[h:], z_mat[1]) + dot(lo[h:], z_mat[1])
    )


def smooth_kernel(
    n, ny, nz,
    source_hbm, guess_hbm, logq_hbm, ry_hbm, rz_hbm, my_hbm, mz_hbm,
    smooth_hbm, all_rhs, coef_hbm, scaled_hbm,
    coef, scaled, ry, rz, my, mz, all_q, q_pad, src, logq, K, U0, U1, U2, D, N, EK, X, H, own, part,
    local_sem, halo_send, halo_recv, part_send, part_recv, q_send, q_recv, r_send, r_recv,
):
    me = lax.axis_index("brick")
    R = ny // CHUNKS
    has = (me > 0, me < n - 1)
    peer_of = (me - 1, me + 1)

    loads = [
        pltpu.make_async_copy(logq_hbm, logq, local_sem.at[0]),
        pltpu.make_async_copy(guess_hbm, U0.at[pl.ds(1, 4), pl.ds(8, ny)], local_sem.at[1]),
        pltpu.make_async_copy(source_hbm, src, local_sem.at[2]),
        pltpu.make_async_copy(my_hbm, my, local_sem.at[3]),
        pltpu.make_async_copy(mz_hbm, mz, local_sem.at[4]),
        pltpu.make_async_copy(ry_hbm, ry, local_sem.at[5]),
        pltpu.make_async_copy(rz_hbm, rz, local_sem.at[6]),
    ]
    for copy in loads:
        copy.start()

    barrier = pltpu.get_barrier_semaphore()

    def greet(k, _):
        pl.semaphore_signal(
            barrier, inc=1, device_id={"brick": lax.rem(me + k, n)}, device_id_type=MESH
        )
        return 0

    lax.fori_loop(1, n, greet, 0)
    pl.semaphore_wait(barrier, n - 1)

    def halo(which, side, c):
        plane = 3 * side
        start = c * R if isinstance(c, int) else pl.multiple_of(c * R, R)
        rows = pl.ds(start, R)
        if which == 2:
            ref = U1.at[plane + 1, pl.ds(start + 8, R)]
        else:
            ref = (logq_hbm, guess_hbm)[which].at[plane, rows]
        return pltpu.make_async_remote_copy(
            src_ref=ref,
            dst_ref=H.at[which, 1 - side, rows],
            send_sem=halo_send.at[which, side, c],
            recv_sem=halo_recv.at[which, 1 - side, c],
            device_id={"brick": peer_of[side]},
            device_id_type=MESH,
        )

    def arrival(which, side, c):
        start = c * R if isinstance(c, int) else pl.multiple_of(c * R, R)
        ref = H.at[which, side, pl.ds(start, R)]
        return pltpu.make_async_remote_copy(
            src_ref=ref,
            dst_ref=ref,
            send_sem=halo_send.at[which, side, c],
            recv_sem=halo_recv.at[which, side, c],
            device_id={"brick": peer_of[side]},
            device_id_type=MESH,
        )

    for c in range(CHUNKS):
        for side in range(2):

            @pl.when(has[side])
            def _():
                halo(0, side, c).start()
                halo(1, side, c).start()

    zero_plane = jnp.zeros((ny + 16, nz), F32)
    zero_rows = jnp.zeros((8, nz), F32)
    for ref in (K, U0, U1, U2):
        ref[0] = zero_plane
        ref[5] = zero_plane
        for p in range(1, 5):
            ref[p, 0:8] = zero_rows
            ref[p, ny + 8 : ny + 16] = zero_rows

    def yz(window):
        size = window.shape[0] - 16
        lane = lax.broadcasted_iota(jnp.int32, (size, nz), 1)
        center = window[8 : size + 8]
        low = jnp.where(lane == 0, 0.0, pltpu.roll(center, 1, 1))
        high = jnp.where(lane == nz - 1, 0.0, pltpu.roll(center, nz - 1, 1))
        return (window[7 : size + 7] + window[9 : size + 9]) + (low + high)

    loads[0].wait()

    def exps(i, _):
        p, start = i // CHUNKS, pl.multiple_of((i % CHUNKS) * R, R)
        K[p + 1, pl.ds(start + 8, R)] = jnp.exp(logq[p, pl.ds(start, R)])
        return 0

    lax.fori_loop(0, 4 * CHUNKS, exps, 0)
    for copy in loads[1:]:
        copy.wait()

    def nearby(U, p, start, size=R):
        at = pl.ds(start + 8, size)
        window = pl.ds(start, size + 16)
        u, k = U[p + 1, window], K[p + 1, window]
        um, up, km, kp = U[p, at], U[p + 2, at], K[p, at], K[p + 2, at]
        su = yz(u) + (um + up)
        sku = yz(u * k) + (km * um + kp * up)
        q = k[8 : size + 8]
        return u[8 : size + 8], q, k, km + kp, 0.5 * (q * su + sku)

    def sweep_one(i, _):
        p, start = i // (CHUNKS // 2), pl.multiple_of((i % (CHUNKS // 2)) * 2 * R, 2 * R)
        rows = pl.ds(start, 2 * R)
        u, q, k, kx, near = nearby(U0, p, start, 2 * R)
        d = 3.0 * q + 0.5 * (yz(k) + kx)
        total = src[p, rows] + near
        D[p, rows] = d
        N[p, rows] = total
        U1[p + 1, pl.ds(start + 8, 2 * R)] = 0.2 * u + 0.8 * total / d
        return 0

    lax.fori_loop(0, 2 * CHUNKS, sweep_one, 0)

    own[...] = to_coarse(
        my[...], mz, (K[1, 8 : ny + 8] + K[2, 8 : ny + 8]) + (K[3, 8 : ny + 8] + K[4, 8 : ny + 8])
    ) * (1.0 / 64.0)
    all_q[me] = own[...]

    def finish_one(c, _):
        start = pl.multiple_of(c * R, R)
        rows, at = pl.ds(start, R), pl.ds(start + 8, R)
        for side in range(2):
            p = 3 * side

            @pl.when(has[side])
            def _():
                arrival(0, side, c).wait_recv()
                arrival(1, side, c).wait_recv()
                q = K[p + 1, at]
                kh = jnp.exp(H[0, side, rows])
                EK[side, rows] = kh
                D[p, rows] = D[p, rows] + 0.5 * kh
                N[p, rows] = N[p, rows] + 0.5 * (q + kh) * H[1, side, rows]

            @pl.when(jnp.logical_not(has[side]))
            def _():
                EK[side, rows] = jnp.zeros((R, nz), F32)

            U1[p + 1, at] = 0.2 * U0[p + 1, at] + 0.8 * N[p, rows] / D[p, rows]

            @pl.when(has[side])
            def _():
                halo(2, side, c).start()

        return 0

    def spread(block, ref, k, send, recv):
        return pltpu.make_async_remote_copy(
            src_ref=block,
            dst_ref=ref.at[me],
            send_sem=send.at[k],
            recv_sem=recv.at[me],
            device_id={"brick": lax.rem(me + k, n)},
            device_id_type=MESH,
        )

    def landed(ref, k, send, recv):
        who = lax.rem(me + k, n)
        return pltpu.make_async_remote_copy(
            src_ref=ref.at[who],
            dst_ref=ref.at[who],
            send_sem=send.at[k],
            recv_sem=recv.at[who],
            device_id={"brick": who},
            device_id_type=MESH,
        )

    def send_q(k, _):
        spread(all_q.at[me], all_q, k, q_send, q_recv).start()
        return 0

    def sweep_two(p, start):
        rows = pl.ds(start, R)
        u, q, k, kx, near = nearby(U1, p, start)
        total = src[p, rows] + near
        N[p, rows] = total
        U2[p + 1, pl.ds(start + 8, R)] = 0.2 * u + 0.8 * total / D[p, rows]
        return 0

    def first_stage(c, _):
        @pl.when(c < CHUNKS)
        def _():
            finish_one(c, 0)

        @pl.when(c == CHUNKS - 1)
        def _():
            lax.fori_loop(1, n, send_q, 0)

        @pl.when(c > 0)
        def _():
            start = pl.multiple_of((c - 1) * R, R)
            lax.fori_loop(0, 4, lambda p, _: sweep_two(p, start), 0)

        return 0

    lax.fori_loop(0, CHUNKS + 1, first_stage, 0)

    def finish_two(c, _):
        start = pl.multiple_of(c * R, R)
        rows, at = pl.ds(start, R), pl.ds(start + 8, R)
        for side in range(2):
            p = 3 * side

            @pl.when(has[side])
            def _():
                arrival(2, side, c).wait_recv()
                total = N[p, rows] + 0.5 * (K[p + 1, at] + EK[side, rows]) * H[2, side, rows]
                U2[p + 1, at] = 0.2 * U1[p + 1, at] + 0.8 * total / D[p, rows]

        return 0

    present = [jnp.where(flag, 0.5, 0.0).astype(F32) for flag in has]

    def residual(c, _):
        start = pl.multiple_of(c * R, R)
        rows, at = pl.ds(start, R), pl.ds(start + 8, R)

        def row(p):
            u, q, k, kx, near = nearby(U2, p, start)
            return src[p, rows] - D[p, rows] * u + near

        r0, r1 = row(0), row(1)
        flo = present[0] * (K[1, at] + EK[0, rows]) * U2[1, at]
        X[0, rows] = 0.625 * flo + 0.375 * r0 + 0.125 * r1
        X[1, rows] = 0.375 * flo + 0.625 * r0 + 0.875 * r1
        r2, r3 = row(2), row(3)
        fhi = present[1] * (K[4, at] + EK[1, rows]) * U2[4, at]
        X[2, rows] = 0.625 * fhi + 0.375 * r3 + 0.125 * r2
        X[1, rows] = X[1, rows] + (0.375 * fhi + 0.625 * r3 + 0.875 * r2)
        return 0

    def second_stage(c, _):
        @pl.when(c < CHUNKS)
        def _():
            finish_two(c, 0)

        @pl.when(c > 0)
        def _():
            residual(c - 1, 0)

        return 0

    lax.fori_loop(0, CHUNKS + 1, second_stage, 0)

    stores = [
        pltpu.make_async_copy(U2.at[pl.ds(1, 4), pl.ds(8, ny)], smooth_hbm, local_sem.at[0]),
        pltpu.make_async_copy(own, all_rhs.at[me], local_sem.at[1]),
        pltpu.make_async_copy(coef, coef_hbm, local_sem.at[2]),
        pltpu.make_async_copy(scaled, scaled_hbm, local_sem.at[3]),
    ]
    stores[0].start()

    def partial(side):
        return pltpu.make_async_remote_copy(
            src_ref=part.at[side],
            dst_ref=part.at[3 - side],
            send_sem=part_send.at[side],
            recv_sem=part_recv.at[1 - side],
            device_id={"brick": peer_of[side]},
            device_id_type=MESH,
        )

    def partial_in(side):
        return pltpu.make_async_remote_copy(
            src_ref=part.at[2 + side],
            dst_ref=part.at[2 + side],
            send_sem=part_send.at[side],
            recv_sem=part_recv.at[side],
            device_id={"brick": peer_of[side]},
            device_id_type=MESH,
        )

    for side in range(2):
        part[side] = to_coarse(ry[...], rz, X[2 * side])

    for side in range(2):

        @pl.when(has[side])
        def _():
            partial(side).start()

    own[...] = to_coarse(ry[...], rz, X[1])
    for side in range(2):

        @pl.when(has[side])
        def _():
            partial_in(side).wait_recv()
            own[...] = own[...] + part[2 + side]

    own[...] = own[...] * (1.0 / 64.0)
    stores[1].start()

    def send_r(k, _):
        spread(own, all_rhs, k, r_send, r_recv).start()
        return 0

    lax.fori_loop(1, n, send_r, 0)

    def settle_q(k, _):
        landed(all_q, k, q_send, q_recv).wait_recv()
        spread(all_q.at[me], all_q, k, q_send, q_recv).wait_send()
        return 0

    def settle_r(k, _):
        landed(all_rhs, k, r_send, r_recv).wait_recv()
        spread(own, all_rhs, k, r_send, r_recv).wait_send()
        return 0

    lax.fori_loop(1, n, settle_q, 0)
    coarse_coefficients(n, min(8, n), all_q, q_pad, coef, scaled)
    stores[2].start()
    stores[3].start()

    for side in range(2):

        @pl.when(has[side])
        def _():
            for c in range(CHUNKS):
                for which in range(3):
                    halo(which, side, c).wait_send()
            partial(side).wait_send()

    lax.fori_loop(1, n, settle_r, 0)
    for copy in stores:
        copy.wait()


def coarse_shifts(shape):
    rows, lanes = shape[1:]
    cz = lanes // 2
    row = lax.broadcasted_iota(jnp.int32, shape, 1)
    lane = lax.broadcasted_iota(jnp.int32, shape, 2)
    low_half = lane < cz
    z = jnp.where(low_half, lane, lane - cz)
    outside = (
        (row == 0) & low_half,
        (row == rows - 1) & jnp.logical_not(low_half),
        z == 0,
        z == cz - 1,
    )

    def shifts(c):
        swapped = pltpu.roll(c, cz, 2)
        y_low = jnp.where(low_half, pltpu.roll(swapped, 1, 1), swapped)
        y_high = jnp.where(low_half, swapped, pltpu.roll(swapped, rows - 1, 1))
        return y_low, y_high, pltpu.roll(c, 1, 2), pltpu.roll(c, lanes - 1, 2)

    return shifts, outside


def coarse_coefficients(n, group, perm, q_pad, coef, scaled):
    rows, lanes = perm.shape[1:]
    shifts, outside = coarse_shifts((group, rows, lanes))
    edge = jnp.zeros((rows, lanes), F32)
    q_pad[0] = edge
    q_pad[n + 1] = edge
    q_pad[1 : n + 1] = perm[...]

    def prepare(g, _):
        at = pl.multiple_of(g * group, group)
        q = q_pad[pl.ds(at + 1, group)]
        near = [q_pad[pl.ds(at, group)], q_pad[pl.ds(at + 2, group)]]
        near += [jnp.where(out, 0.0, v) for out, v in zip(outside, shifts(q))]
        faces = [0.5 * (q + v) for v in near]
        diagonal = ((faces[0] + faces[1]) + (faces[2] + faces[3])) + (faces[4] + faces[5])
        scale = 0.8 / diagonal
        for k, out in enumerate((None, None) + outside):
            f = faces[k] * scale
            coef[k, pl.ds(at, group)] = f if out is None else jnp.where(out, 0.0, f)
        scaled[pl.ds(at, group)] = 16.0 * scale
        return 0

    lax.fori_loop(0, n // group, prepare, 0)


def coarse_kernel(
    n, group,
    owner_hbm, rhs_hbm, coef_hbm, scaled_hbm, smooth_hbm, ez_hbm, ey_hbm,
    corrected_hbm, held,
    owner, rhs, coef, scaled, smooth, ez, ey, C, B, corrected, sem,
):
    me = lax.axis_index("brick")
    loads = [
        pltpu.make_async_copy(*pair, sem.at[4 + k])
        for k, pair in enumerate(
            (
                (rhs_hbm, rhs), (scaled_hbm, scaled), (coef_hbm, coef),
                (ez_hbm, ez), (ey_hbm, ey), (smooth_hbm, smooth), (owner_hbm, owner),
            )
        )
    ]
    for load in loads:
        load.start()
    rows, lanes = rhs.shape[1:]
    shifts, _ = coarse_shifts((group, rows, lanes))
    edge = jnp.zeros((rows, lanes), F32)
    for slot in range(2):
        C[slot, 0] = edge
        C[slot, n + 1] = edge
    loads[0].wait()
    loads[1].wait()
    B[...] = rhs[...] * scaled[...]
    C[0, 1 : n + 1] = B[...]

    loads[2].wait()
    for sweep in range(SWEEPS - 1):
        now, later = sweep % 2, 1 - sweep % 2

        def step(g, _):
            at = pl.multiple_of(g * group, group)
            c = C[now, pl.ds(at + 1, group)]
            near = (C[now, pl.ds(at, group)], C[now, pl.ds(at + 2, group)]) + shifts(c)
            terms = [coef[k, pl.ds(at, group)] * v for k, v in enumerate(near)]
            total = B[pl.ds(at, group)] + 0.2 * c
            total = (total + (terms[0] + terms[1])) + ((terms[2] + terms[3]) + (terms[4] + terms[5]))
            C[later, pl.ds(at + 1, group)] = total
            return 0

        lax.fori_loop(0, n // group, step, 0)

    final = (SWEEPS - 1) % 2

    for load in loads[3:]:
        load.wait()
    below, mid, above = C[final, me], C[final, me + 1], C[final, me + 2]
    planes = jnp.concatenate(
        [
            0.625 * mid + 0.375 * below,
            0.875 * mid + 0.125 * below,
            0.875 * mid + 0.125 * above,
            0.625 * mid + 0.375 * above,
        ],
        axis=0,
    )
    hi, lo = split(planes)
    even = dot(hi, ez[0]) + dot(lo, ez[0])
    odd = dot(hi, ez[1]) + dot(lo, ez[1])
    for p in range(4):
        both = jnp.concatenate(
            [even[p * rows : (p + 1) * rows], odd[p * rows : (p + 1) * rows]], axis=0
        )
        hi, lo = split(both)
        corrected[p] = smooth[p] + (dot(ey[...], hi) + dot(ey[...], lo))
        pltpu.make_async_copy(corrected.at[p], corrected_hbm.at[p], sem.at[p]).start()

    mine = jnp.zeros((rows, lanes), F32)
    for b in range(n):
        mine = jnp.where(owner[b] == me, C[final, b + 1], mine)
    for r in range(rows):
        held[0:1, r * lanes : (r + 1) * lanes] = mine[r : r + 1]
    for p in range(4):
        pltpu.make_async_copy(corrected.at[p], corrected_hbm.at[p], sem.at[p]).wait()


def local(n, source, guess, log_perm, owner):
    planes, ny, nz = source.shape
    assert planes == 4
    cells = (ny // 4) * (nz // 4)
    rows, lanes = ny // 8, nz // 2
    dense = (rows, lanes)
    as_bf16 = lambda m: jnp.asarray(m.astype(ml_dtypes.bfloat16))
    py, pz = even_odd(prolong_matrix(ny)), prolong_matrix(nz)
    ry, rz = as_bf16(py.T), as_bf16(halves(pz))
    my, mz = as_bf16(even_odd(mean_matrix(ny)).T), as_bf16(halves(mean_matrix(nz)))
    ey, ez = as_bf16(py), as_bf16(halves(pz).transpose(0, 2, 1))
    vmem = pl.BlockSpec(memory_space=pltpu.VMEM)
    hbm = pl.BlockSpec(memory_space=pl.ANY)
    whole = lambda *s: pltpu.VMEM(s, F32)
    dma = lambda *s: pltpu.SemaphoreType.DMA(s)
    padded = (6, ny + 16, nz)
    smooth, all_rhs, coef, scaled = pl.pallas_call(
        functools.partial(smooth_kernel, n, ny, nz),
        out_shape=(
            jax.ShapeDtypeStruct((4, ny, nz), F32),
            jax.ShapeDtypeStruct((n,) + dense, F32),
            jax.ShapeDtypeStruct((6, n) + dense, F32),
            jax.ShapeDtypeStruct((n,) + dense, F32),
        ),
        in_specs=[hbm] * 7,
        out_specs=(hbm,) * 4,
        scratch_shapes=[
            whole(6, n, *dense), whole(n, *dense),
            pltpu.VMEM(ry.shape, BF16), pltpu.VMEM(rz.shape, BF16),
            pltpu.VMEM(my.shape, BF16), pltpu.VMEM(mz.shape, BF16),
            whole(n, *dense), whole(n + 2, *dense),
            whole(4, ny, nz), whole(4, ny, nz),
            whole(*padded), whole(*padded), whole(*padded), whole(*padded),
            whole(4, ny, nz), whole(4, ny, nz),
            whole(2, ny, nz), whole(3, ny, nz), whole(3, 2, ny, nz),
            whole(*dense), whole(4, *dense),
            dma(7), dma(3, 2, CHUNKS), dma(3, 2, CHUNKS), dma(2), dma(2),
            dma(n), dma(n), dma(n), dma(n),
        ],
        compiler_params=pltpu.CompilerParams(
            collective_id=0, has_side_effects=True, vmem_limit_bytes=60 * 2**20
        ),
        name="smooth",
    )(source, guess, log_perm, ry, rz, my, mz)
    return pl.pallas_call(
        functools.partial(coarse_kernel, n, min(16, n)),
        out_shape=(
            jax.ShapeDtypeStruct((4, ny, nz), F32),
            jax.ShapeDtypeStruct((1, cells), F32),
        ),
        in_specs=[hbm] * 7,
        out_specs=(hbm, vmem),
        scratch_shapes=[
            pltpu.SMEM((n,), jnp.int32),
            whole(n, *dense), whole(6, n, *dense), whole(n, *dense), whole(4, ny, nz),
            pltpu.VMEM(ez.shape, BF16), pltpu.VMEM(ey.shape, BF16),
            whole(2, n + 2, *dense), whole(n, *dense), whole(4, ny, nz), dma(11),
        ],
        compiler_params=pltpu.CompilerParams(vmem_limit_bytes=60 * 2**20),
        name="coarse",
    )(owner, all_rhs, coef, scaled, smooth, ez, ey)


def solution(mesh):
    spec = P(("samples", "brick"), None, None)
    return jax.shard_map(
        functools.partial(local, mesh.shape["brick"]),
        mesh=mesh,
        in_specs=(spec, spec, spec, P()),
        out_specs=(spec, P(("samples", "brick"), None)),
        check_vma=False,
    )
```
